32 devices in a mesh: row: 8 (over y, x, core), col: 4 (over z).
Axes of the slice: x: 2, y: 2, z: 4, core: 2. Of those that a mesh axis runs over, the one named last changes fastest.
Arguments:
- ancestor_inverse: bfloat16 [2048, 2048], P('row', 'col'), may hold values from -6 to 6
- panel_one: bfloat16 [2048, 512], P(('row', 'col')), may hold values from -0.125 to 0.125
- ancestors_one: int32 [2, 7], replicated, may hold values from 0 to 7, as said below
- diag_inverse_one: bfloat16 [2, 256, 256], replicated, may hold values from -6 to 6
- panel_two: bfloat16 [2048, 512], P(('row', 'col')), may hold values from -0.125 to 0.125
- link_two: bfloat16 [2, 256, 256], replicated, may hold values from -0.375 to 0.375
- ancestors_two: int32 [2, 6], replicated, may hold values from 0 to 7, as said below
- diag_inverse_two: bfloat16 [2, 256, 256], replicated, may hold values from -6 to 6
- widths: int32 [4], replicated, may hold values from 128 to 256, as said below
Outputs:
- column_one: bfloat16 [2048, 512], P(('row', 'col'))
- block_one: bfloat16 [2, 256, 256], replicated
- column_two: bfloat16 [2048, 512], P(('row', 'col'))
- parent_rows_two: bfloat16 [2, 256, 256], replicated
- block_two: bfloat16 [2, 256, 256], replicated
The draws below stay inside these ranges and needn't reach their ends.
Inputs may be any that keep to these rules, and one draw needn't show every extreme that they name: `ancestors_one`: each row lists 7 distinct tiles in ascending order; 0 and 7 are always among them. `ancestors_two`: row s lists 6 distinct entries of row s of ancestors_one in ascending order; 0 and 7 are always among them. `widths`: at least one supernode uses all 256 columns.
All inputs are finite; a program needn't handle non-finite values.
Results may differ from the reference program's by a relative error of at most 0.0055.
Values may be sent and summed in bfloat16 or wider, within the bound.
A program may use at most 64 MiB of HBM per device.

```python
import jax
import jax.numpy as jnp

W = 256
TILES = 8
M = 2048
R_ONE = 7
R_TWO = 6


def ancestor_rows(key):
    base_key = jax.random.fold_in(key, 11)
    chosen_rows = []
    for sibling in range(2):
        sibling_key = jax.random.fold_in(base_key, sibling)
        middle_rows = jax.random.permutation(sibling_key, TILES - 2)[:R_ONE - 2].astype(jnp.int32) + 1
        picked = jnp.concatenate([jnp.zeros((1,), jnp.int32), middle_rows, jnp.full((1,), TILES - 1, jnp.int32)])
        chosen_rows.append(jnp.sort(picked))
    return jnp.stack(chosen_rows).astype(jnp.int32)


def draw_ancestors_one(key, part):
    return ancestor_rows(key)


def draw_ancestors_two(key, part):
    parent_rows = ancestor_rows(key)
    base_key = jax.random.fold_in(key, 23)
    chosen_rows = []
    for sibling in range(2):
        sibling_key = jax.random.fold_in(base_key, sibling)
        middle_index = jax.random.permutation(sibling_key, R_ONE - 2)[:R_TWO - 2].astype(jnp.int32) + 1
        picked = jnp.concatenate([parent_rows[sibling, 0:1], parent_rows[sibling][middle_index], parent_rows[sibling, R_ONE - 1:R_ONE]])
        chosen_rows.append(jnp.sort(picked))
    return jnp.stack(chosen_rows).astype(jnp.int32)


def draw_widths(key, part):
    width_key = jax.random.fold_in(key, 31)
    place_key = jax.random.fold_in(key, 37)
    drawn_widths = jax.random.randint(width_key, (4,), W // 2, W + 1, dtype=jnp.int32)
    full_index = jax.random.randint(place_key, (), 0, 4, dtype=jnp.int32)
    return jnp.where(jnp.arange(4, dtype=jnp.int32) == full_index, W, drawn_widths).astype(jnp.int32)


def spiked(result, stream_key, source, target, shards_of, factor):
    def block_of(dim):
        return (jnp.arange(result.shape[dim]) // (result.shape[dim] // shards_of)).reshape((-1,) + (1,) * (result.ndim - 1 - dim))

    first = jax.random.permutation(stream_key, shards_of)[block_of(target)]
    second = (block_of(target) + shards_of // 2) % shards_of
    return jnp.where((block_of(source) == first) | (block_of(source) == second), factor * result, result)


def shard_levels(own_key, dims, shards, low, largest):
    level = 1.0
    for position, shards_of in shards:
        heights = jax.random.uniform(jax.random.fold_in(jax.random.fold_in(own_key, 6), position), (shards_of,), jnp.float32, low / len(shards), largest / len(shards))
        level = level * jnp.repeat(jnp.exp(heights), dims[position] // shards_of).reshape((-1,) + (1,) * (len(dims) - 1 - position))
    return level


def normal_values(rng, extent, spread, limit, split=(), held_as=jnp.bfloat16):
    drawn = jax.random.normal(rng, extent, jnp.float32) * spread
    if len(split) > 0:
        drawn = shard_levels(rng, extent, split, -0.22, 0.18) * drawn
    return jnp.clip(drawn, min=-limit, max=limit).astype(held_as)


def bell_draw_with(own_key, shape, deviation, bound, shards, heavy, kind=jnp.bfloat16):
    array = deviation * jax.random.normal(own_key, shape, jnp.float32)
    if shards:
        array = array * shard_levels(own_key, shape, shards, -0.22, 0.18)
    return jnp.clip(spiked(array, jax.random.fold_in(own_key, 3), *heavy), -bound, bound).astype(kind)


def setup_inputs(seed: int = 0) -> dict:
    key_list = jax.random.split(jax.random.key(seed), 10)
    ancestor_inverse = bell_draw_with(key_list[0], (M, M), 1.0, 6.0, ((0, 8), (1, 4)), (1, 0, 8, 2.0))
    panel_one = normal_values(key_list[1], (M, 2 * W), M ** -0.5, 0.125, ((0, 32),))
    ancestors_one = draw_ancestors_one(jax.random.fold_in(key_list[9], 71), 0)
    diag_inverse_one = normal_values(key_list[3], (2, W, W), 1.0, 6.0)
    panel_two = normal_values(key_list[4], (M, 2 * W), M ** -0.5, 0.125, ((0, 32),))
    link_two = normal_values(key_list[5], (2, W, W), W ** -0.5, 0.375)
    ancestors_two = draw_ancestors_two(jax.random.fold_in(key_list[9], 71), 0)
    diag_inverse_two = normal_values(key_list[7], (2, W, W), 1.0, 6.0)
    widths = draw_widths(jax.random.fold_in(key_list[9], 71), 0)
    return {"ancestor_inverse": ancestor_inverse, "panel_one": panel_one, "ancestors_one": ancestors_one, "diag_inverse_one": diag_inverse_one, "panel_two": panel_two, "link_two": link_two, "ancestors_two": ancestors_two, "diag_inverse_two": diag_inverse_two, "widths": widths}


def row_members(ancestors, tile_count, tile_width):
    tile_ids = jnp.arange(tile_count, dtype=jnp.int32)
    matches = (ancestors[:, :, None] == tile_ids[None, None, :]).astype(jnp.int32)
    member = jnp.sum(matches, axis=1)
    return jnp.repeat(member, tile_width, axis=1).astype(jnp.bfloat16)


def reference(ancestor_inverse, panel_one, ancestors_one, diag_inverse_one, panel_two, link_two, ancestors_two, diag_inverse_two, widths):
    tile_width = diag_inverse_one.shape[-1]
    matrix_order = ancestor_inverse.shape[0]
    tile_count = matrix_order // tile_width
    columns = jnp.arange(tile_width, dtype=jnp.int32)
    keep_columns = (columns[None, :] < widths[:, None]).astype(jnp.bfloat16)
    member_one = row_members(ancestors_one, tile_count, tile_width)
    member_two = row_members(ancestors_two, tile_count, tile_width)
    mask_one = (member_one.T[:, :, None] * keep_columns[0:2][None, :, :]).reshape(matrix_order, 2 * tile_width)
    mask_two = (member_two.T[:, :, None] * keep_columns[2:4][None, :, :]).reshape(matrix_order, 2 * tile_width)
    lower_one = panel_one * mask_one
    lower_two = panel_two * mask_two
    product = jnp.dot(ancestor_inverse, jnp.concatenate([lower_one, lower_two], axis=1), preferred_element_type=jnp.float32)
    columns_first = []
    blocks_first = []
    columns_second = []
    parent_blocks = []
    blocks_second = []
    for sibling in range(2):
        low = sibling * tile_width
        high = (sibling + 1) * tile_width
        keep_parent = keep_columns[sibling]
        keep_child = keep_columns[2 + sibling]
        pivot_one = diag_inverse_one[sibling].astype(jnp.float32) * (keep_parent[:, None] * keep_parent[None, :]).astype(jnp.float32)
        pivot_two = diag_inverse_two[sibling].astype(jnp.float32) * (keep_child[:, None] * keep_child[None, :]).astype(jnp.float32)
        link_masked = link_two[sibling] * keep_parent[:, None] * keep_child[None, :]
        lower_first = lower_one[:, low:high]
        lower_second = lower_two[:, low:high]
        column_first = (-(product[:, low:high] * member_one[sibling][:, None].astype(jnp.float32))).astype(jnp.bfloat16)
        block_first = (pivot_one - jnp.dot(lower_first.T, column_first, preferred_element_type=jnp.float32)).astype(jnp.bfloat16)
        second_total = product[:, 2 * tile_width + low:2 * tile_width + high] + jnp.dot(column_first, link_masked, preferred_element_type=jnp.float32)
        column_second = (-(second_total * member_two[sibling][:, None].astype(jnp.float32))).astype(jnp.bfloat16)
        cross_total = jnp.dot(column_first.T, lower_second, preferred_element_type=jnp.float32)
        parent_block = (-(jnp.dot(block_first, link_masked, preferred_element_type=jnp.float32) + cross_total)).astype(jnp.bfloat16)
        lower_total = jnp.dot(lower_second.T, column_second, preferred_element_type=jnp.float32)
        block_second = (pivot_two - jnp.dot(link_masked.T, parent_block, preferred_element_type=jnp.float32) - lower_total).astype(jnp.bfloat16)
        columns_first.append(column_first)
        blocks_first.append(block_first)
        columns_second.append(column_second)
        parent_blocks.append(parent_block)
        blocks_second.append(block_second)
    return (jnp.concatenate(columns_first, axis=1), jnp.stack(blocks_first), jnp.concatenate(columns_second, axis=1), jnp.stack(parent_blocks), jnp.stack(blocks_second))
```

```python
import functools

import jax
import jax.numpy as jnp
from jax import lax
from jax.experimental import pallas as pl
from jax.experimental.pallas import tpu as pltpu
from jax.sharding import PartitionSpec as P

MESH = pl.DeviceIdType.MESH
PIECES = 4
F32 = jnp.float32
BF16 = jnp.bfloat16


def left_t(a, b):
    return lax.dot_general(a, b, (((0,), (0,)), ((), ())), preferred_element_type=F32)


def kernel(
    n,
    depth,
    panel_one,
    panel_two,
    anc_one,
    anc_two,
    widths,
    inv_hbm,
    diag_one_hbm,
    diag_two_hbm,
    link_hbm,
    col_one_out,
    block_one_out,
    col_two_out,
    parent_out,
    block_two_out,
    inv,
    diag_one,
    diag_two,
    link,
    lines,
    relay,
    panels,
    prod,
    prod_send,
    prod_recv,
    pair_send,
    pair_recv,
    sums,
    plane_send,
    plane_recv,
    part,
    line_send,
    line_recv,
    whole,
    load_sem,
    a_sem,
    b_sem,
    c_send,
    c_recv,
    f_send,
    f_recv,
    l_sem,
    p_sem,
    pair_sem,
    ps_sem,
    ls_sem,
    lg_sem,
    pg_sem,
    fg_sem,
):
    width = diag_one.shape[-1]
    share = panel_one.shape[0]
    small = n == PIECES
    row = lax.axis_index("row")
    z = lax.axis_index("col")
    chip = row // 2
    core = row % 2
    mine = chip % PIECES
    group = chip - mine
    z_group = z - z % PIECES
    sibling = (2 * chip + (1 - core), z)

    def on_chip(c):
        return (2 * c + core, z)

    def on_line(level):
        return (row, level)

    def send(src, dst, ssem, rsem, target):
        copy = pltpu.make_async_remote_copy(
            src_ref=src, dst_ref=dst, send_sem=ssem, recv_sem=rsem, device_id=target, device_id_type=MESH
        )
        copy.start()
        return copy

    def arrived(dst, rsem):
        pltpu.make_async_copy(dst, dst, rsem).wait()

    loads = []
    for i, (src, dst) in enumerate(
        ((inv_hbm, inv), (link_hbm, link), (diag_one_hbm, diag_one), (diag_two_hbm, diag_two))
    ):
        loads.append(pltpu.make_async_copy(src, dst, load_sem.at[i]))
        loads[-1].start()

    barrier = pltpu.get_barrier_semaphore()
    pl.semaphore_signal(barrier, inc=1, device_id=sibling, device_id_type=MESH)
    for i in range(1, n):
        pl.semaphore_signal(barrier, inc=1, device_id=on_chip((chip + i) % n), device_id_type=MESH)
    for i in range(1, depth):
        pl.semaphore_signal(barrier, inc=1, device_id=on_line((z + i) % depth), device_id_type=MESH)

    columns = lax.broadcasted_iota(jnp.int32, (share, width), 1)
    member = []
    for p in range(PIECES):
        ancestors, s = (anc_one, p) if p < 2 else (anc_two, p - 2)
        found = jnp.int32(0)
        for t in range(ancestors.shape[1]):
            found += jnp.where(ancestors[s, t] == row, 1, 0).astype(jnp.int32)
        member.append(found.astype(F32))
        source = panel_one if p < 2 else panel_two
        values = source[:, s * width : (s + 1) * width]
        kept = jnp.where(columns < widths[p] * found, values.astype(F32), 0.0).astype(BF16)
        lines[z, p] = kept
    relay[mine] = lines[z, mine]

    pl.semaphore_wait(barrier, 1 + (n - 1) + (depth - 1))

    sent = []
    copies = []
    for i in range(1, PIECES):
        p = (mine + i) % PIECES
        copies.append(
            send(lines.at[z, p], relay.at[mine], a_sem.at[0, i], a_sem.at[1, i], on_chip(group + p))
        )
    for copy in copies:
        copy.wait_recv()
    sent += copies
    is_relay = group == z_group

    def local_piece():
        panels[mine, core, z] = relay[z % PIECES]

    if small:
        local_piece()
        first = None
    else:
        first = pltpu.make_async_remote_copy(
            src_ref=relay.at[z % PIECES],
            dst_ref=panels.at[mine, core, z],
            send_sem=b_sem.at[0, 0],
            recv_sem=b_sem.at[1, z],
            device_id=on_line(group + z % PIECES),
            device_id_type=MESH,
        )
        pl.when(is_relay)(local_piece)
        pl.when(jnp.logical_not(is_relay))(first.start)
    for i in range(1, PIECES):
        j = (z + i) % PIECES
        sent.append(
            send(relay.at[j], panels.at[mine, core, z], b_sem.at[0, i], b_sem.at[1, z], on_line(group + j))
        )
    line_copies = []

    def share_line():
        for i in range(1, depth):
            line_copies.append(
                send(lines.at[z], lines.at[z], l_sem.at[0, i], l_sem.at[1, z], on_line((z + i) % depth))
            )

    chunks = [(z + i) % depth for i in range(depth)] if small else [None]

    def chunk(p, c, level):
        return panels.at[p, c] if level is None else panels.at[p, c, level]

    def slot(level):
        return 0 if level is None else level

    def spread(start):
        for t, level in enumerate(chunks):
            if start:
                if level is None:
                    for i in range(1, depth):
                        other = (z + i) % depth
                        arrived(panels.at[mine, core, other], b_sem.at[1, other])
                elif t > 0:
                    arrived(panels.at[mine, core, level], b_sem.at[1, level])
            here = chunk(mine, core, level)
            targets = [(on_chip((chip + i) % n), c_recv) for i in range(1, n)] + [(sibling, f_recv)]
            for i, (target, rsem) in enumerate(targets):
                copy = pltpu.make_async_remote_copy(
                    src_ref=here,
                    dst_ref=here,
                    send_sem=c_send.at[t, i],
                    recv_sem=rsem.at[mine, slot(level)],
                    device_id=target,
                    device_id_type=MESH,
                )
                if start:
                    copy.start()
                else:
                    copy.wait_send()
            if start and small and t == 0:
                share_line()

    if small:
        spread(True)
    else:
        share_line()
        pl.when(is_relay)(functools.partial(spread, True))

    def forward(p, start):
        for t, level in enumerate(chunks):
            here = chunk(p, core, level)
            if start:
                arrived(here, c_recv.at[p, slot(level)])
            copy = pltpu.make_async_remote_copy(
                src_ref=here,
                dst_ref=here,
                send_sem=f_send.at[p, t],
                recv_sem=f_recv.at[p, slot(level)],
                device_id=sibling,
                device_id_type=MESH,
            )
            if start:
                copy.start()
            else:
                copy.wait_send()

    if not small:
        pl.when(jnp.logical_not(is_relay))(functools.partial(forward, mine, True))
    if small:
        for t, level in enumerate(chunks):
            for i in range(1, PIECES):
                p = (mine + i) % PIECES
                here = chunk(p, core, level)
                arrived(here, c_recv.at[p, level])
                sent.append(send(here, here, f_send.at[p, t], f_recv.at[p, level], sibling))
    else:
        for i in range(1, PIECES):
            forward((mine + i) % PIECES, True)
    for copy in loads:
        copy.wait()
    for p in range(PIECES):
        for level in range(depth if small else 1):
            arrived(chunk(p, 1 - core, level if small else None), f_recv.at[p, level])

    for p in range(PIECES):
        stacked = panels[p].reshape(2 * depth * share, width)
        product = jnp.dot(inv[...], stacked, preferred_element_type=F32) * member[p]
        prod[p] = product
        prod_send[:, p] = product.astype(BF16).reshape(depth, share, width)
    for i in range(1, depth):
        other = (z + i) % depth
        sent.append(
            send(prod_send.at[other], prod_recv.at[z], p_sem.at[0, i], p_sem.at[1, z], on_line(other))
        )
    for i in range(1, depth):
        other = (z + i) % depth
        arrived(lines.at[other], l_sem.at[1, other])

    def square(ref, p):
        return ref[:, p].reshape(depth * share, width)

    def inner(s):
        first_lower, second_lower = square(lines, s), square(lines, 2 + s)
        first, second = square(prod_send, s), square(prod_send, 2 + s)
        return left_t(first_lower, first), left_t(second_lower, first), left_t(second_lower, second)

    for m, value in enumerate(inner(1 - core)):
        pair_send[m] = value.astype(BF16)
    pair = send(pair_send, pair_recv, pair_sem.at[0], pair_sem.at[1], sibling)
    sent.append(pair)
    for m, value in enumerate(inner(core)):
        sums[m] = value
    pair.wait_recv()

    rows = width // n
    for m in range(3):
        value = sums[m] + pair_recv[m].astype(F32)
        sums[m] = value
        plane_send[:, m] = value.astype(BF16).reshape(n, rows, width)
    for i in range(1, n):
        other = (chip + i) % n
        sent.append(
            send(plane_send.at[other], plane_recv.at[chip], ps_sem.at[0, i], ps_sem.at[1, chip], on_chip(other))
        )
    first_row = pl.multiple_of(chip * rows, rows)
    for i in range(1, n):
        other = (chip + i) % n
        arrived(plane_recv.at[other], ps_sem.at[1, other])
    for m in range(3):
        value = sums[m, pl.ds(first_row, rows)]
        for i in range(1, n):
            value += plane_recv[(chip + i) % n, m].astype(F32)
        part[m] = value

    owners = line_send.shape[0]
    owned = rows // owners
    for m in range(3):
        line_send[:, m] = part[m].astype(BF16).reshape(owners, owned, width)
    every = owners == depth

    def line_part(copy_at, start):
        if every:
            return
        for t in range(owners):
            copy = copy_at(t, t)

            @pl.when(z != t)
            def _():
                if start:
                    copy.start()
                else:
                    copy.wait_send()

    def reduce_copy(t, i):
        return pltpu.make_async_remote_copy(
            src_ref=line_send.at[t],
            dst_ref=line_recv.at[z],
            send_sem=ls_sem.at[0, i],
            recv_sem=ls_sem.at[1, z],
            device_id=on_line(t),
            device_id_type=MESH,
        )

    if every:
        for i in range(1, depth):
            copy = reduce_copy((z + i) % depth, i)
            copy.start()
            sent.append(copy)
    line_part(reduce_copy, True)

    def owned_rows(level):
        return pl.ds(pl.multiple_of(chip * rows + level * owned, owned), owned)

    def gather_copy(i):
        here = whole.at[core, :, owned_rows(z), :]
        return pltpu.make_async_remote_copy(
            src_ref=here,
            dst_ref=here,
            send_sem=lg_sem.at[0, i],
            recv_sem=lg_sem.at[1, z],
            device_id=on_line((z + i) % depth),
            device_id_type=MESH,
        )

    def own():
        for i in range(1, depth):
            other = (z + i) % depth
            arrived(line_recv.at[other], ls_sem.at[1, other])
        local = pl.ds(pl.multiple_of(z * owned, owned), owned)
        limit = widths[core]
        at = chip * rows + z * owned + lax.broadcasted_iota(jnp.int32, (owned, width), 0)
        across = lax.broadcasted_iota(jnp.int32, (owned, width), 1)
        for m in range(3):
            value = part[m, local]
            for i in range(1, depth):
                value += line_recv[(z + i) % depth, m].astype(F32)
            if m == 0:
                pivot = diag_one[core, owned_rows(z)].astype(F32)
                value += jnp.where((at < limit) & (across < limit), pivot, 0.0)
            whole[core, m, owned_rows(z)] = value.astype(BF16)
        for i in range(1, depth):
            gather_copy(i).start()

    def own_end():
        for i in range(1, depth):
            gather_copy(i).wait_send()

    if every:
        own()
    else:
        pl.when(z < owners)(own)

    if every:
        for i in range(1, depth):
            level = (z + i) % depth
            arrived(whole.at[core, :, owned_rows(level), :], lg_sem.at[1, level])
    else:
        for t in range(owners):

            @pl.when(z != t)
            def _():
                arrived(whole.at[core, :, owned_rows(t), :], lg_sem.at[1, t])

    def chip_rows(c, s):
        return whole.at[s, :, pl.ds(pl.multiple_of(c * rows, rows), rows), :]

    here = chip_rows(chip, core)
    for i in range(1, n):
        sent.append(send(here, here, pg_sem.at[0, i], pg_sem.at[1, chip], on_chip((chip + i) % n)))
    sent.append(send(here, here, fg_sem.at[0, chip], fg_sem.at[1, chip], sibling))

    for i in range(1, depth):
        other = (z + i) % depth
        arrived(prod_recv.at[other], p_sem.at[1, other])

    def masked_link(s):
        at = lax.broadcasted_iota(jnp.int32, (width, width), 0)
        across = lax.broadcasted_iota(jnp.int32, (width, width), 1)
        kept = (at < widths[s]) & (across < widths[2 + s])
        return jnp.where(kept, link[s].astype(F32), 0.0).astype(BF16)

    links = [masked_link(s) for s in range(2)]
    totals = []
    for p in range(PIECES):
        value = prod[p, pl.ds(pl.multiple_of(z * share, share), share)]
        for i in range(1, depth):
            value += prod_recv[(z + i) % depth, p].astype(F32)
        totals.append(value)
    for s in range(2):
        new = (-totals[s]).astype(BF16)
        col_one_out[:, s * width : (s + 1) * width] = new
        second = totals[2 + s] + jnp.dot(new, links[s], preferred_element_type=F32)
        col_two_out[:, s * width : (s + 1) * width] = (-(second * member[2 + s])).astype(BF16)

    for i in range(1, n):
        other = (chip + i) % n
        there = chip_rows(other, core)
        arrived(there, pg_sem.at[1, other])
        sent.append(send(there, there, fg_sem.at[0, other], fg_sem.at[1, other], sibling))
    for c in range(n):
        arrived(chip_rows(c, 1 - core), fg_sem.at[1, c])

    for s in range(2):
        block = whole[s, 0]
        cross = whole[s, 1]
        block_one_out[s] = block
        parent = cross.astype(F32).T - jnp.dot(block, links[s], preferred_element_type=F32)
        parent = parent.astype(BF16)
        parent_out[s] = parent
        at = lax.broadcasted_iota(jnp.int32, (width, width), 0)
        across = lax.broadcasted_iota(jnp.int32, (width, width), 1)
        limit = widths[2 + s]
        value = jnp.where((at < limit) & (across < limit), diag_two[s].astype(F32), 0.0)
        value += whole[s, 2].astype(F32)
        value -= jnp.dot(cross, links[s], preferred_element_type=F32)
        value -= left_t(links[s], parent)
        block_two_out[s] = value.astype(BF16)

    for copy in sent + line_copies:
        copy.wait_send()
    line_part(reduce_copy, False)
    if small:
        spread(False)
    else:
        pl.when(jnp.logical_not(is_relay))(first.wait_send)
        pl.when(is_relay)(functools.partial(spread, False))
        pl.when(jnp.logical_not(is_relay))(functools.partial(forward, mine, False))
        for i in range(1, PIECES):
            forward((mine + i) % PIECES, False)
    if every:
        own_end()
    else:
        pl.when(z < owners)(own_end)


def solution(mesh):
    n = mesh.shape["row"] // 2
    depth = mesh.shape["col"]

    def local(inverse, panel_one, anc_one, diag_one, panel_two, link_two, anc_two, diag_two, widths):
        width = diag_one.shape[-1]
        share = panel_one.shape[0]
        rows = width // n
        owners = max(1, min(depth, rows // 16))
        assert inverse.shape == (width, 2 * width) and n == depth and n % PIECES == 0
        assert share * depth == width and panel_one.shape[1] == 2 * width
        chunks = depth if n == PIECES else 1
        vmem = pl.BlockSpec(memory_space=pltpu.VMEM)
        smem = pl.BlockSpec(memory_space=pltpu.SMEM)
        hbm = pl.BlockSpec(memory_space=pl.ANY)
        dma = pltpu.SemaphoreType.DMA
        square = (2, width, width)
        return pl.pallas_call(
            functools.partial(kernel, n, depth),
            out_shape=(
                jax.ShapeDtypeStruct(panel_one.shape, BF16),
                jax.ShapeDtypeStruct(square, BF16),
                jax.ShapeDtypeStruct(panel_two.shape, BF16),
                jax.ShapeDtypeStruct(square, BF16),
                jax.ShapeDtypeStruct(square, BF16),
            ),
            in_specs=[vmem, vmem, smem, smem, smem, hbm, hbm, hbm, hbm],
            out_specs=[vmem] * 5,
            scratch_shapes=[
                pltpu.VMEM(inverse.shape, BF16),
                pltpu.VMEM(square, BF16),
                pltpu.VMEM(square, BF16),
                pltpu.VMEM(square, BF16),
                pltpu.VMEM((depth, PIECES, share, width), BF16),
                pltpu.VMEM((PIECES, share, width), BF16),
                pltpu.VMEM((PIECES, 2, depth, share, width), BF16),
                pltpu.VMEM((PIECES, width, width), F32),
                pltpu.VMEM((depth, PIECES, share, width), BF16),
                pltpu.VMEM((depth, PIECES, share, width), BF16),
                pltpu.VMEM((3, width, width), BF16),
                pltpu.VMEM((3, width, width), BF16),
                pltpu.VMEM((3, width, width), F32),
                pltpu.VMEM((n, 3, rows, width), BF16),
                pltpu.VMEM((n, 3, rows, width), BF16),
                pltpu.VMEM((3, rows, width), F32),
                pltpu.VMEM((owners, 3, rows // owners, width), BF16),
                pltpu.VMEM((depth, 3, rows // owners, width), BF16),
                pltpu.VMEM((2, 3, width, width), BF16),
                dma((4,)),
                dma((2, PIECES)),
                dma((2, max(depth, PIECES))),
                dma((chunks, n)),
                dma((PIECES, chunks)),
                dma((PIECES, chunks)),
                dma((PIECES, chunks)),
                dma((2, depth)),
                dma((2, depth)),
                dma((2,)),
                dma((2, n)),
                dma((2, depth)),
                dma((2, depth)),
                dma((2, n)),
                dma((2, n)),
            ],
            compiler_params=pltpu.CompilerParams(
                collective_id=0, has_side_effects=True, vmem_limit_bytes=40 * 1024 * 1024
            ),
            cost_estimate=pl.CostEstimate(flops=10**9, bytes_accessed=3 * 10**6, transcendentals=0),
        )(panel_one, panel_two, anc_one, anc_two, widths, inverse, diag_one, diag_two, link_two)

    in_specs = (
        P("row", "col"),
        P(("row", "col"), None),
        P(),
        P(),
        P(("row", "col"), None),
        P(),
        P(),
        P(),
        P(),
    )
    out_specs = (P(("row", "col"), None), P(), P(("row", "col"), None), P(), P())
    return jax.shard_map(local, mesh=mesh, in_specs=in_specs, out_specs=out_specs, check_vma=False)
```

```python
import functools

import jax
import jax.numpy as jnp
from jax import lax
from jax.experimental import pallas as pl
from jax.experimental.pallas import tpu as pltpu
from jax.sharding import PartitionSpec as P

MESH = pl.DeviceIdType.MESH
PIECES = 4
F32 = jnp.float32
BF16 = jnp.bfloat16


def left_t(a, b):
    return lax.dot_general(a, b, (((0,), (0,)), ((), ())), preferred_element_type=F32)


def hand_over(*refs):
    copies = [pltpu.make_async_copy(refs[i], refs[5 + i], refs[10].at[i]) for i in range(5)]
    for copy in copies:
        copy.start()
    for copy in copies:
        copy.wait()


def kernel(
    n,
    depth,
    panel_one_hbm,
    panel_two_hbm,
    anc_one_hbm,
    anc_two_hbm,
    widths_hbm,
    inv_hbm,
    diag_one_hbm,
    diag_two_hbm,
    link_hbm,
    col_one_out,
    block_one_out,
    col_two_out,
    parent_out,
    block_two_out,
    panel_one,
    panel_two,
    anc_one,
    anc_two,
    widths,
    inv,
    diag_one,
    diag_two,
    link,
    lines,
    relay,
    panels,
    prod,
    prod_send,
    prod_recv,
    pair_send,
    pair_recv,
    sums,
    plane_send,
    plane_recv,
    part,
    line_send,
    line_recv,
    whole,
    load_sem,
    a_sem,
    b_sem,
    c_send,
    c_recv,
    f_send,
    f_recv,
    l_sem,
    p_sem,
    pair_sem,
    ps_sem,
    ls_sem,
    lg_sem,
    pg_sem,
    fg_sem,
):
    width = diag_one.shape[-1]
    share = panel_one.shape[0]
    small = n == PIECES
    row = lax.axis_index("row")
    z = lax.axis_index("col")
    chip = row // 2
    core = row % 2
    mine = chip % PIECES
    group = chip - mine
    z_group = z - z % PIECES
    sibling = (2 * chip + (1 - core), z)

    def on_chip(c):
        return (2 * c + core, z)

    def on_line(level):
        return (row, level)

    def send(src, dst, ssem, rsem, target):
        copy = pltpu.make_async_remote_copy(
            src_ref=src, dst_ref=dst, send_sem=ssem, recv_sem=rsem, device_id=target, device_id_type=MESH
        )
        copy.start()
        return copy

    def arrived(dst, rsem):
        pltpu.make_async_copy(dst, dst, rsem).wait()

    loads = []
    pairs = (
        (anc_one_hbm, anc_one),
        (anc_two_hbm, anc_two),
        (widths_hbm, widths),
        (panel_one_hbm, panel_one),
        (panel_two_hbm, panel_two),
        (inv_hbm, inv),
        (link_hbm, link),
        (diag_one_hbm, diag_one),
        (diag_two_hbm, diag_two),
    )
    for i, (src, dst) in enumerate(pairs):
        loads.append(pltpu.make_async_copy(src, dst, load_sem.at[i]))
        loads[-1].start()

    barrier = pltpu.get_barrier_semaphore()
    pl.semaphore_signal(barrier, inc=1, device_id=sibling, device_id_type=MESH)
    for i in range(1, n):
        pl.semaphore_signal(barrier, inc=1, device_id=on_chip((chip + i) % n), device_id_type=MESH)
    for i in range(1, depth):
        pl.semaphore_signal(barrier, inc=1, device_id=on_line((z + i) % depth), device_id_type=MESH)

    for copy in loads[:5]:
        copy.wait()
    columns = lax.broadcasted_iota(jnp.int32, (share, width), 1)
    member = []
    for p in range(PIECES):
        ancestors, s = (anc_one, p) if p < 2 else (anc_two, p - 2)
        found = jnp.int32(0)
        for t in range(ancestors.shape[1]):
            found += jnp.where(ancestors[s, t] == row, 1, 0).astype(jnp.int32)
        member.append(found.astype(F32))
        source = panel_one if p < 2 else panel_two
        values = source[:, s * width : (s + 1) * width]
        kept = jnp.where(columns < widths[p] * found, values.astype(F32), 0.0).astype(BF16)
        lines[z, p] = kept
    relay[mine] = lines[z, mine]

    pl.semaphore_wait(barrier, 1 + (n - 1) + (depth - 1))

    sent = []
    copies = []
    for i in range(1, PIECES):
        p = (mine + i) % PIECES
        copies.append(
            send(lines.at[z, p], relay.at[mine], a_sem.at[0, i], a_sem.at[1, i], on_chip(group + p))
        )
    for copy in copies:
        copy.wait_recv()
    sent += copies
    is_relay = group == z_group

    def local_piece():
        panels[mine, core, z] = relay[z % PIECES]

    if small:
        local_piece()
        first = None
    else:
        first = pltpu.make_async_remote_copy(
            src_ref=relay.at[z % PIECES],
            dst_ref=panels.at[mine, core, z],
            send_sem=b_sem.at[0, 0],
            recv_sem=b_sem.at[1, z],
            device_id=on_line(group + z % PIECES),
            device_id_type=MESH,
        )
        pl.when(is_relay)(local_piece)
        pl.when(jnp.logical_not(is_relay))(first.start)
    for i in range(1, PIECES):
        j = (z + i) % PIECES
        sent.append(
            send(relay.at[j], panels.at[mine, core, z], b_sem.at[0, i], b_sem.at[1, z], on_line(group + j))
        )
    line_copies = []

    def share_line():
        for i in range(1, depth):
            line_copies.append(
                send(lines.at[z], lines.at[z], l_sem.at[0, i], l_sem.at[1, z], on_line((z + i) % depth))
            )

    chunks = [(z + i) % depth for i in range(depth)] if small else [None]

    def chunk(p, c, level):
        return panels.at[p, c] if level is None else panels.at[p, c, level]

    def slot(level):
        return 0 if level is None else level

    def spread(start):
        for t, level in enumerate(chunks):
            if start:
                if level is None:
                    for i in range(1, depth):
                        other = (z + i) % depth
                        arrived(panels.at[mine, core, other], b_sem.at[1, other])
                elif t > 0:
                    arrived(panels.at[mine, core, level], b_sem.at[1, level])
            here = chunk(mine, core, level)
            targets = [(on_chip((chip + i) % n), c_recv) for i in range(1, n)] + [(sibling, f_recv)]
            for i, (target, rsem) in enumerate(targets):
                copy = pltpu.make_async_remote_copy(
                    src_ref=here,
                    dst_ref=here,
                    send_sem=c_send.at[t, i],
                    recv_sem=rsem.at[mine, slot(level)],
                    device_id=target,
                    device_id_type=MESH,
                )
                if start:
                    copy.start()
                else:
                    copy.wait_send()
            if start and small and t == 0:
                share_line()

    if small:
        spread(True)
    else:
        share_line()
        pl.when(is_relay)(functools.partial(spread, True))

    def forward(p, start):
        for t, level in enumerate(chunks):
            here = chunk(p, core, level)
            if start:
                arrived(here, c_recv.at[p, slot(level)])
            copy = pltpu.make_async_remote_copy(
                src_ref=here,
                dst_ref=here,
                send_sem=f_send.at[p, t],
                recv_sem=f_recv.at[p, slot(level)],
                device_id=sibling,
                device_id_type=MESH,
            )
            if start:
                copy.start()
            else:
                copy.wait_send()

    if not small:
        pl.when(jnp.logical_not(is_relay))(functools.partial(forward, mine, True))
    if small:
        for t, level in enumerate(chunks):
            for i in range(1, PIECES):
                p = (mine + i) % PIECES
                here = chunk(p, core, level)
                arrived(here, c_recv.at[p, level])
                sent.append(send(here, here, f_send.at[p, t], f_recv.at[p, level], sibling))
    else:
        for i in range(1, PIECES):
            forward((mine + i) % PIECES, True)
    for copy in loads[5:]:
        copy.wait()
    for p in range(PIECES):
        for level in range(depth if small else 1):
            arrived(chunk(p, 1 - core, level if small else None), f_recv.at[p, level])

    for p in range(PIECES):
        stacked = panels[p].reshape(2 * depth * share, width)
        product = jnp.dot(inv[...], stacked, preferred_element_type=F32) * member[p]
        prod[p] = product
        prod_send[:, p] = product.astype(BF16).reshape(depth, share, width)
    for i in range(1, depth):
        other = (z + i) % depth
        sent.append(
            send(prod_send.at[other], prod_recv.at[z], p_sem.at[0, i], p_sem.at[1, z], on_line(other))
        )
    for i in range(1, depth):
        other = (z + i) % depth
        arrived(lines.at[other], l_sem.at[1, other])

    def square(ref, p):
        return ref[:, p].reshape(depth * share, width)

    def inner(s):
        first_lower, second_lower = square(lines, s), square(lines, 2 + s)
        first, second = square(prod_send, s), square(prod_send, 2 + s)
        return left_t(first_lower, first), left_t(second_lower, first), left_t(second_lower, second)

    for m, value in enumerate(inner(1 - core)):
        pair_send[m] = value.astype(BF16)
    pair = send(pair_send, pair_recv, pair_sem.at[0], pair_sem.at[1], sibling)
    sent.append(pair)
    for m, value in enumerate(inner(core)):
        sums[m] = value
    pair.wait_recv()

    rows = width // n
    for m in range(3):
        value = sums[m] + pair_recv[m].astype(F32)
        sums[m] = value
        plane_send[:, m] = value.astype(BF16).reshape(n, rows, width)
    for i in range(1, n):
        other = (chip + i) % n
        sent.append(
            send(plane_send.at[other], plane_recv.at[chip], ps_sem.at[0, i], ps_sem.at[1, chip], on_chip(other))
        )
    first_row = pl.multiple_of(chip * rows, rows)
    for i in range(1, n):
        other = (chip + i) % n
        arrived(plane_recv.at[other], ps_sem.at[1, other])
    for m in range(3):
        value = sums[m, pl.ds(first_row, rows)]
        for i in range(1, n):
            value += plane_recv[(chip + i) % n, m].astype(F32)
        part[m] = value

    owners = line_send.shape[0]
    owned = rows // owners
    for m in range(3):
        line_send[:, m] = part[m].astype(BF16).reshape(owners, owned, width)
    every = owners == depth

    def line_part(copy_at, start):
        if every:
            return
        for t in range(owners):
            copy = copy_at(t, t)

            @pl.when(z != t)
            def _():
                if start:
                    copy.start()
                else:
                    copy.wait_send()

    def reduce_copy(t, i):
        return pltpu.make_async_remote_copy(
            src_ref=line_send.at[t],
            dst_ref=line_recv.at[z],
            send_sem=ls_sem.at[0, i],
            recv_sem=ls_sem.at[1, z],
            device_id=on_line(t),
            device_id_type=MESH,
        )

    if every:
        for i in range(1, depth):
            copy = reduce_copy((z + i) % depth, i)
            copy.start()
            sent.append(copy)
    line_part(reduce_copy, True)

    def owned_rows(level):
        return pl.ds(pl.multiple_of(chip * rows + level * owned, owned), owned)

    def gather_copy(i):
        here = whole.at[core, :, owned_rows(z), :]
        return pltpu.make_async_remote_copy(
            src_ref=here,
            dst_ref=here,
            send_sem=lg_sem.at[0, i],
            recv_sem=lg_sem.at[1, z],
            device_id=on_line((z + i) % depth),
            device_id_type=MESH,
        )

    def own():
        for i in range(1, depth):
            other = (z + i) % depth
            arrived(line_recv.at[other], ls_sem.at[1, other])
        local = pl.ds(pl.multiple_of(z * owned, owned), owned)
        limit = widths[core]
        at = chip * rows + z * owned + lax.broadcasted_iota(jnp.int32, (owned, width), 0)
        across = lax.broadcasted_iota(jnp.int32, (owned, width), 1)
        for m in range(3):
            value = part[m, local]
            for i in range(1, depth):
                value += line_recv[(z + i) % depth, m].astype(F32)
            if m == 0:
                pivot = diag_one[core, owned_rows(z)].astype(F32)
                value += jnp.where((at < limit) & (across < limit), pivot, 0.0)
            whole[core, m, owned_rows(z)] = value.astype(BF16)
        for i in range(1, depth):
            gather_copy(i).start()

    def own_end():
        for i in range(1, depth):
            gather_copy(i).wait_send()

    if every:
        own()
    else:
        pl.when(z < owners)(own)

    if every:
        for i in range(1, depth):
            level = (z + i) % depth
            arrived(whole.at[core, :, owned_rows(level), :], lg_sem.at[1, level])
    else:
        for t in range(owners):

            @pl.when(z != t)
            def _():
                arrived(whole.at[core, :, owned_rows(t), :], lg_sem.at[1, t])

    def chip_rows(c, s):
        return whole.at[s, :, pl.ds(pl.multiple_of(c * rows, rows), rows), :]

    here = chip_rows(chip, core)
    for i in range(1, n):
        sent.append(send(here, here, pg_sem.at[0, i], pg_sem.at[1, chip], on_chip((chip + i) % n)))
    sent.append(send(here, here, fg_sem.at[0, chip], fg_sem.at[1, chip], sibling))

    for i in range(1, depth):
        other = (z + i) % depth
        arrived(prod_recv.at[other], p_sem.at[1, other])

    def masked_link(s):
        at = lax.broadcasted_iota(jnp.int32, (width, width), 0)
        across = lax.broadcasted_iota(jnp.int32, (width, width), 1)
        kept = (at < widths[s]) & (across < widths[2 + s])
        return jnp.where(kept, link[s].astype(F32), 0.0).astype(BF16)

    links = [masked_link(s) for s in range(2)]
    totals = []
    for p in range(PIECES):
        value = prod[p, pl.ds(pl.multiple_of(z * share, share), share)]
        for i in range(1, depth):
            value += prod_recv[(z + i) % depth, p].astype(F32)
        totals.append(value)
    for s in range(2):
        new = (-totals[s]).astype(BF16)
        col_one_out[:, s * width : (s + 1) * width] = new
        second = totals[2 + s] + jnp.dot(new, links[s], preferred_element_type=F32)
        col_two_out[:, s * width : (s + 1) * width] = (-(second * member[2 + s])).astype(BF16)

    for i in range(1, n):
        other = (chip + i) % n
        there = chip_rows(other, core)
        arrived(there, pg_sem.at[1, other])
        sent.append(send(there, there, fg_sem.at[0, other], fg_sem.at[1, other], sibling))
    for c in range(n):
        arrived(chip_rows(c, 1 - core), fg_sem.at[1, c])

    for s in range(2):
        block = whole[s, 0]
        cross = whole[s, 1]
        block_one_out[s] = block
        parent = cross.astype(F32).T - jnp.dot(block, links[s], preferred_element_type=F32)
        parent = parent.astype(BF16)
        parent_out[s] = parent
        at = lax.broadcasted_iota(jnp.int32, (width, width), 0)
        across = lax.broadcasted_iota(jnp.int32, (width, width), 1)
        limit = widths[2 + s]
        value = jnp.where((at < limit) & (across < limit), diag_two[s].astype(F32), 0.0)
        value += whole[s, 2].astype(F32)
        value -= jnp.dot(cross, links[s], preferred_element_type=F32)
        value -= left_t(links[s], parent)
        block_two_out[s] = value.astype(BF16)

    for copy in sent + line_copies:
        copy.wait_send()
    line_part(reduce_copy, False)
    if small:
        spread(False)
    else:
        pl.when(jnp.logical_not(is_relay))(first.wait_send)
        pl.when(is_relay)(functools.partial(spread, False))
        pl.when(jnp.logical_not(is_relay))(functools.partial(forward, mine, False))
        for i in range(1, PIECES):
            forward((mine + i) % PIECES, False)
    if every:
        own_end()
    else:
        pl.when(z < owners)(own_end)


def solution(mesh):
    n = mesh.shape["row"] // 2
    depth = mesh.shape["col"]

    def local(inverse, panel_one, anc_one, diag_one, panel_two, link_two, anc_two, diag_two, widths):
        width = diag_one.shape[-1]
        share = panel_one.shape[0]
        rows = width // n
        owners = max(1, min(depth, rows // 16))
        assert inverse.shape == (width, 2 * width) and n == depth and n % PIECES == 0
        assert share * depth == width and panel_one.shape[1] == 2 * width
        chunks = depth if n == PIECES else 1
        vmem = pl.BlockSpec(memory_space=pltpu.VMEM)
        hbm = pl.BlockSpec(memory_space=pl.ANY)
        dma = pltpu.SemaphoreType.DMA
        square = (2, width, width)
        results = pl.pallas_call(
            functools.partial(kernel, n, depth),
            out_shape=(
                jax.ShapeDtypeStruct(panel_one.shape, BF16),
                jax.ShapeDtypeStruct(square, BF16),
                jax.ShapeDtypeStruct(panel_two.shape, BF16),
                jax.ShapeDtypeStruct(square, BF16),
                jax.ShapeDtypeStruct(square, BF16),
            ),
            in_specs=[hbm] * 9,
            out_specs=[vmem] * 5,
            scratch_shapes=[
                pltpu.VMEM(panel_one.shape, BF16),
                pltpu.VMEM(panel_two.shape, BF16),
                pltpu.SMEM(anc_one.shape, jnp.int32),
                pltpu.SMEM(anc_two.shape, jnp.int32),
                pltpu.SMEM(widths.shape, jnp.int32),
                pltpu.VMEM(inverse.shape, BF16),
                pltpu.VMEM(square, BF16),
                pltpu.VMEM(square, BF16),
                pltpu.VMEM(square, BF16),
                pltpu.VMEM((depth, PIECES, share, width), BF16),
                pltpu.VMEM((PIECES, share, width), BF16),
                pltpu.VMEM((PIECES, 2, depth, share, width), BF16),
                pltpu.VMEM((PIECES, width, width), F32),
                pltpu.VMEM((depth, PIECES, share, width), BF16),
                pltpu.VMEM((depth, PIECES, share, width), BF16),
                pltpu.VMEM((3, width, width), BF16),
                pltpu.VMEM((3, width, width), BF16),
                pltpu.VMEM((3, width, width), F32),
                pltpu.VMEM((n, 3, rows, width), BF16),
                pltpu.VMEM((n, 3, rows, width), BF16),
                pltpu.VMEM((3, rows, width), F32),
                pltpu.VMEM((owners, 3, rows // owners, width), BF16),
                pltpu.VMEM((depth, 3, rows // owners, width), BF16),
                pltpu.VMEM((2, 3, width, width), BF16),
                dma((9,)),
                dma((2, PIECES)),
                dma((2, max(depth, PIECES))),
                dma((chunks, n)),
                dma((PIECES, chunks)),
                dma((PIECES, chunks)),
                dma((PIECES, chunks)),
                dma((2, depth)),
                dma((2, depth)),
                dma((2,)),
                dma((2, n)),
                dma((2, depth)),
                dma((2, depth)),
                dma((2, n)),
                dma((2, n)),
            ],
            compiler_params=pltpu.CompilerParams(
                collective_id=0, has_side_effects=True, vmem_limit_bytes=60 * 1024 * 1024
            ),
            cost_estimate=pl.CostEstimate(flops=10**9, bytes_accessed=3 * 10**6, transcendentals=0),
        )(panel_one, panel_two, anc_one, anc_two, widths, inverse, diag_one, diag_two, link_two)
        return pl.pallas_call(
            hand_over,
            out_shape=tuple(jax.ShapeDtypeStruct(r.shape, r.dtype) for r in results),
            in_specs=[hbm] * 5,
            out_specs=[hbm] * 5,
            scratch_shapes=[dma((5,))],
            compiler_params=pltpu.CompilerParams(vmem_limit_bytes=60 * 1024 * 1024),
        )(*results)

    in_specs = (
        P("row", "col"),
        P(("row", "col"), None),
        P(),
        P(),
        P(("row", "col"), None),
        P(),
        P(),
        P(),
        P(),
    )
    out_specs = (P(("row", "col"), None), P(), P(("row", "col"), None), P(), P())
    return jax.shard_map(local, mesh=mesh, in_specs=in_specs, out_specs=out_specs, check_vma=False)
```

```python
import functools

import jax
import jax.numpy as jnp
from jax import lax
from jax.experimental import pallas as pl
from jax.experimental.pallas import tpu as pltpu
from jax.sharding import PartitionSpec as P

MESH = pl.DeviceIdType.MESH
PIECES = 4
F32 = jnp.float32
BF16 = jnp.bfloat16


def left_t(a, b):
    return lax.dot_general(a, b, (((0,), (0,)), ((), ())), preferred_element_type=F32)


def hand_over(*refs):
    sources, targets, held, sem = refs[:5], refs[5:10], refs[10:15], refs[15]
    loads = [pltpu.make_async_copy(sources[i], held[i], sem.at[0, i]) for i in range(5)]
    stores = [pltpu.make_async_copy(held[i], targets[i], sem.at[1, i]) for i in range(5)]
    for copy in loads:
        copy.start()
    for load, store in zip(loads, stores):
        load.wait()
        store.start()
    for copy in stores:
        copy.wait()


def kernel(
    n,
    depth,
    panel_one_hbm,
    panel_two_hbm,
    anc_one_hbm,
    anc_two_hbm,
    widths_hbm,
    inv_hbm,
    diag_one_hbm,
    diag_two_hbm,
    link_hbm,
    col_one_out,
    block_one_out,
    col_two_out,
    parent_out,
    block_two_out,
    panel_one,
    panel_two,
    anc_one,
    anc_two,
    widths,
    inv,
    diag_one,
    diag_two,
    link,
    lines,
    relay,
    panels,
    prod,
    prod_send,
    prod_recv,
    pair_send,
    pair_recv,
    sums,
    plane_send,
    plane_recv,
    part,
    line_send,
    line_recv,
    whole,
    load_sem,
    a_sem,
    b_sem,
    c_send,
    c_recv,
    f_send,
    f_recv,
    l_sem,
    p_sem,
    pair_sem,
    ps_sem,
    ls_sem,
    lg_sem,
    pg_sem,
    fg_sem,
):
    width = diag_one.shape[-1]
    share = panel_one.shape[0]
    small = n == PIECES
    row = lax.axis_index("row")
    z = lax.axis_index("col")
    chip = row // 2
    core = row % 2
    mine = chip % PIECES
    group = chip - mine
    z_group = z - z % PIECES
    sibling = (2 * chip + (1 - core), z)

    def on_chip(c):
        return (2 * c + core, z)

    def on_line(level):
        return (row, level)

    def send(src, dst, ssem, rsem, target):
        copy = pltpu.make_async_remote_copy(
            src_ref=src, dst_ref=dst, send_sem=ssem, recv_sem=rsem, device_id=target, device_id_type=MESH
        )
        copy.start()
        return copy

    def arrived(dst, rsem):
        pltpu.make_async_copy(dst, dst, rsem).wait()

    loads = []
    pairs = (
        (anc_one_hbm, anc_one),
        (anc_two_hbm, anc_two),
        (widths_hbm, widths),
        (panel_one_hbm, panel_one),
        (panel_two_hbm, panel_two),
        (inv_hbm, inv),
        (link_hbm, link),
        (diag_one_hbm, diag_one),
        (diag_two_hbm, diag_two),
    )
    for i, (src, dst) in enumerate(pairs):
        loads.append(pltpu.make_async_copy(src, dst, load_sem.at[i]))
        loads[-1].start()

    barrier = pltpu.get_barrier_semaphore()
    pl.semaphore_signal(barrier, inc=1, device_id=sibling, device_id_type=MESH)
    for i in range(1, n):
        pl.semaphore_signal(barrier, inc=1, device_id=on_chip((chip + i) % n), device_id_type=MESH)
    for i in range(1, depth):
        pl.semaphore_signal(barrier, inc=1, device_id=on_line((z + i) % depth), device_id_type=MESH)

    for copy in loads[:5]:
        copy.wait()
    columns = lax.broadcasted_iota(jnp.int32, (share, width), 1)
    member = []
    for p in range(PIECES):
        ancestors, s = (anc_one, p) if p < 2 else (anc_two, p - 2)
        found = jnp.int32(0)
        for t in range(ancestors.shape[1]):
            found += jnp.where(ancestors[s, t] == row, 1, 0).astype(jnp.int32)
        member.append(found.astype(F32))
        source = panel_one if p < 2 else panel_two
        values = source[:, s * width : (s + 1) * width]
        kept = jnp.where(columns < widths[p] * found, values.astype(F32), 0.0).astype(BF16)
        lines[z, p] = kept
    relay[mine] = lines[z, mine]

    pl.semaphore_wait(barrier, 1 + (n - 1) + (depth - 1))

    sent = []
    copies = []
    for i in range(1, PIECES):
        p = (mine + i) % PIECES
        copies.append(
            send(lines.at[z, p], relay.at[mine], a_sem.at[0, i], a_sem.at[1, i], on_chip(group + p))
        )
    for copy in copies:
        copy.wait_recv()
    sent += copies
    is_relay = group == z_group

    def local_piece():
        panels[mine, core, z] = relay[z % PIECES]

    if small:
        local_piece()
        first = None
    else:
        first = pltpu.make_async_remote_copy(
            src_ref=relay.at[z % PIECES],
            dst_ref=panels.at[mine, core, z],
            send_sem=b_sem.at[0, 0],
            recv_sem=b_sem.at[1, z],
            device_id=on_line(group + z % PIECES),
            device_id_type=MESH,
        )
        pl.when(is_relay)(local_piece)
        pl.when(jnp.logical_not(is_relay))(first.start)
    for i in range(1, PIECES):
        j = (z + i) % PIECES
        sent.append(
            send(relay.at[j], panels.at[mine, core, z], b_sem.at[0, i], b_sem.at[1, z], on_line(group + j))
        )
    line_copies = []

    def share_line():
        for i in range(1, depth):
            line_copies.append(
                send(lines.at[z], lines.at[z], l_sem.at[0, i], l_sem.at[1, z], on_line((z + i) % depth))
            )

    chunks = [(z + i) % depth for i in range(depth)] if small else [None]

    def chunk(p, c, level):
        return panels.at[p, c] if level is None else panels.at[p, c, level]

    def slot(level):
        return 0 if level is None else level

    def spread(start):
        for t, level in enumerate(chunks):
            if start:
                if level is None:
                    for i in range(1, depth):
                        other = (z + i) % depth
                        arrived(panels.at[mine, core, other], b_sem.at[1, other])
                elif t > 0:
                    arrived(panels.at[mine, core, level], b_sem.at[1, level])
            here = chunk(mine, core, level)
            targets = [(on_chip((chip + i) % n), c_recv) for i in range(1, n)] + [(sibling, f_recv)]
            for i, (target, rsem) in enumerate(targets):
                copy = pltpu.make_async_remote_copy(
                    src_ref=here,
                    dst_ref=here,
                    send_sem=c_send.at[t, i],
                    recv_sem=rsem.at[mine, slot(level)],
                    device_id=target,
                    device_id_type=MESH,
                )
                if start:
                    copy.start()
                else:
                    copy.wait_send()
            if start and small and t == 0:
                share_line()

    if small:
        spread(True)
    else:
        share_line()
        pl.when(is_relay)(functools.partial(spread, True))

    def forward(p, start):
        for t, level in enumerate(chunks):
            here = chunk(p, core, level)
            if start:
                arrived(here, c_recv.at[p, slot(level)])
            copy = pltpu.make_async_remote_copy(
                src_ref=here,
                dst_ref=here,
                send_sem=f_send.at[p, t],
                recv_sem=f_recv.at[p, slot(level)],
                device_id=sibling,
                device_id_type=MESH,
            )
            if start:
                copy.start()
            else:
                copy.wait_send()

    if not small:
        pl.when(jnp.logical_not(is_relay))(functools.partial(forward, mine, True))
    if small:
        for t, level in enumerate(chunks):
            for i in range(1, PIECES):
                p = (mine + i) % PIECES
                here = chunk(p, core, level)
                arrived(here, c_recv.at[p, level])
                sent.append(send(here, here, f_send.at[p, t], f_recv.at[p, level], sibling))
    else:
        for i in range(1, PIECES):
            forward((mine + i) % PIECES, True)
    for copy in loads[5:]:
        copy.wait()
    for p in range(PIECES):
        for level in range(depth if small else 1):
            arrived(chunk(p, 1 - core, level if small else None), f_recv.at[p, level])

    for p in range(PIECES):
        stacked = panels[p].reshape(2 * depth * share, width)
        product = jnp.dot(inv[...], stacked, preferred_element_type=F32) * member[p]
        prod[p] = product
        prod_send[:, p] = product.astype(BF16).reshape(depth, share, width)
    def send_products(half):
        for i in range(1, depth):
            other = (z + i) % depth
            sent.append(
                send(
                    prod_send.at[other, 2 * half : 2 * half + 2],
                    prod_recv.at[z, 2 * half : 2 * half + 2],
                    p_sem.at[0, half, i],
                    p_sem.at[1, half, z],
                    on_line(other),
                )
            )

    send_products(0)
    for i in range(1, depth):
        other = (z + i) % depth
        arrived(lines.at[other], l_sem.at[1, other])

    def square(ref, p):
        return ref[:, p].reshape(depth * share, width)

    def inner(s, m):
        lower = square(lines, s if m == 0 else 2 + s)
        return left_t(lower, square(prod_send, 2 + s if m == 2 else s))

    rows = width // n
    owners = line_send.shape[1]
    owned = rows // owners
    every = owners == depth
    first_row = pl.multiple_of(chip * rows, rows)

    def pair_start(m):
        pair_send[m] = inner(1 - core, m).astype(BF16)
        sent.append(send(pair_send.at[m], pair_recv.at[m], pair_sem.at[0, m], pair_sem.at[1, m], sibling))

    def plane_start(m):
        value = inner(core, m)
        arrived(pair_recv.at[m], pair_sem.at[1, m])
        value += pair_recv[m].astype(F32)
        sums[m] = value
        plane_send[m] = value.astype(BF16).reshape(n, rows, width)
        for i in range(1, n):
            other = (chip + i) % n
            sent.append(
                send(
                    plane_send.at[m, other],
                    plane_recv.at[m, chip],
                    ps_sem.at[0, m, i],
                    ps_sem.at[1, m, chip],
                    on_chip(other),
                )
            )

    def reduce_copy(m, t, i):
        return pltpu.make_async_remote_copy(
            src_ref=line_send.at[m, t],
            dst_ref=line_recv.at[m, z],
            send_sem=ls_sem.at[0, m, i],
            recv_sem=ls_sem.at[1, m, z],
            device_id=on_line(t),
            device_id_type=MESH,
        )

    def to_owners(m, start):
        for t in range(owners):
            copy = reduce_copy(m, t, t)
            pl.when(z != t)(copy.start if start else copy.wait_send)

    def line_start(m):
        value = sums[m, pl.ds(first_row, rows)]
        for i in range(1, n):
            other = (chip + i) % n
            arrived(plane_recv.at[m, other], ps_sem.at[1, m, other])
            value += plane_recv[m, other].astype(F32)
        part[m] = value
        line_send[m] = value.astype(BF16).reshape(owners, owned, width)
        if every:
            for i in range(1, depth):
                copy = reduce_copy(m, (z + i) % depth, i)
                copy.start()
                sent.append(copy)
        else:
            to_owners(m, True)

    def owned_rows(level):
        return pl.ds(pl.multiple_of(chip * rows + level * owned, owned), owned)

    def gather_copy(m, i):
        here = whole.at[core, m, owned_rows(z), :]
        return pltpu.make_async_remote_copy(
            src_ref=here,
            dst_ref=here,
            send_sem=lg_sem.at[0, m, i],
            recv_sem=lg_sem.at[1, m, z],
            device_id=on_line((z + i) % depth),
            device_id_type=MESH,
        )

    def own(m):
        value = part[m, pl.ds(pl.multiple_of(z * owned, owned), owned)]
        for i in range(1, depth):
            other = (z + i) % depth
            arrived(line_recv.at[m, other], ls_sem.at[1, m, other])
            value += line_recv[m, other].astype(F32)
        if m == 0:
            limit = widths[core]
            at = chip * rows + z * owned + lax.broadcasted_iota(jnp.int32, (owned, width), 0)
            across = lax.broadcasted_iota(jnp.int32, (owned, width), 1)
            pivot = diag_one[core, owned_rows(z)].astype(F32)
            value += jnp.where((at < limit) & (across < limit), pivot, 0.0)
        whole[core, m, owned_rows(z)] = value.astype(BF16)
        for i in range(1, depth):
            gather_copy(m, i).start()

    def own_end(m):
        for i in range(1, depth):
            gather_copy(m, i).wait_send()

    def owners_only(f, m):
        if every:
            f(m)
        else:
            pl.when(z < owners)(functools.partial(f, m))

    def chip_rows(c, s, m):
        return whole.at[s, m, pl.ds(pl.multiple_of(c * rows, rows), rows), :]

    def back_start(m):
        if every:
            for i in range(1, depth):
                level = (z + i) % depth
                arrived(whole.at[core, m, owned_rows(level), :], lg_sem.at[1, m, level])
        else:
            for t in range(owners):
                there = whole.at[core, m, owned_rows(t), :]
                pl.when(z != t)(functools.partial(arrived, there, lg_sem.at[1, m, t]))
        here = chip_rows(chip, core, m)
        for i in range(1, n):
            sent.append(send(here, here, pg_sem.at[0, m, i], pg_sem.at[1, m, chip], on_chip((chip + i) % n)))
        sent.append(send(here, here, fg_sem.at[0, m, chip], fg_sem.at[1, m, chip], sibling))

    def back_forward(m):
        for i in range(1, n):
            other = (chip + i) % n
            there = chip_rows(other, core, m)
            arrived(there, pg_sem.at[1, m, other])
            sent.append(send(there, there, fg_sem.at[0, m, other], fg_sem.at[1, m, other], sibling))

    for m in range(3):
        pair_start(m)
    for m in range(3):
        plane_start(m)
    line_start(0)
    line_start(1)
    owners_only(own, 0)
    line_start(2)
    owners_only(own, 1)
    back_start(0)
    owners_only(own, 2)
    send_products(1)
    back_start(1)
    back_forward(0)
    back_start(2)
    back_forward(1)

    def masked_link(s):
        at = lax.broadcasted_iota(jnp.int32, (width, width), 0)
        across = lax.broadcasted_iota(jnp.int32, (width, width), 1)
        kept = (at < widths[s]) & (across < widths[2 + s])
        return jnp.where(kept, link[s].astype(F32), 0.0).astype(BF16)

    links = [masked_link(s) for s in range(2)]

    def total(p):
        value = prod[p, pl.ds(pl.multiple_of(z * share, share), share)]
        for i in range(1, depth):
            value += prod_recv[(z + i) % depth, p].astype(F32)
        return value

    def products_arrived(half):
        for i in range(1, depth):
            other = (z + i) % depth
            arrived(prod_recv.at[other, 2 * half : 2 * half + 2], p_sem.at[1, half, other])

    products_arrived(0)
    added = []
    for s in range(2):
        new = (-total(s)).astype(BF16)
        col_one_out[:, s * width : (s + 1) * width] = new
        added.append(jnp.dot(new, links[s], preferred_element_type=F32))
    back_forward(2)
    products_arrived(1)
    for s in range(2):
        second = total(2 + s) + added[s]
        col_two_out[:, s * width : (s + 1) * width] = (-(second * member[2 + s])).astype(BF16)
    for m in range(3):
        for c in range(n):
            arrived(chip_rows(c, 1 - core, m), fg_sem.at[1, m, c])

    for s in range(2):
        block = whole[s, 0]
        cross = whole[s, 1]
        block_one_out[s] = block
        parent = cross.astype(F32).T - jnp.dot(block, links[s], preferred_element_type=F32)
        parent = parent.astype(BF16)
        parent_out[s] = parent
        at = lax.broadcasted_iota(jnp.int32, (width, width), 0)
        across = lax.broadcasted_iota(jnp.int32, (width, width), 1)
        limit = widths[2 + s]
        value = jnp.where((at < limit) & (across < limit), diag_two[s].astype(F32), 0.0)
        value += whole[s, 2].astype(F32)
        value -= jnp.dot(cross, links[s], preferred_element_type=F32)
        value -= left_t(links[s], parent)
        block_two_out[s] = value.astype(BF16)

    for copy in sent + line_copies:
        copy.wait_send()
    if small:
        spread(False)
    else:
        pl.when(jnp.logical_not(is_relay))(first.wait_send)
        pl.when(is_relay)(functools.partial(spread, False))
        pl.when(jnp.logical_not(is_relay))(functools.partial(forward, mine, False))
        for i in range(1, PIECES):
            forward((mine + i) % PIECES, False)
    for m in range(3):
        if not every:
            to_owners(m, False)
        owners_only(own_end, m)


def solution(mesh):
    n = mesh.shape["row"] // 2
    depth = mesh.shape["col"]

    def local(inverse, panel_one, anc_one, diag_one, panel_two, link_two, anc_two, diag_two, widths):
        width = diag_one.shape[-1]
        share = panel_one.shape[0]
        rows = width // n
        owners = max(1, min(depth, rows // 16))
        assert inverse.shape == (width, 2 * width) and n == depth and n % PIECES == 0
        assert share * depth == width and panel_one.shape[1] == 2 * width
        chunks = depth if n == PIECES else 1
        vmem = pl.BlockSpec(memory_space=pltpu.VMEM)
        hbm = pl.BlockSpec(memory_space=pl.ANY)
        dma = pltpu.SemaphoreType.DMA
        square = (2, width, width)
        results = pl.pallas_call(
            functools.partial(kernel, n, depth),
            out_shape=(
                jax.ShapeDtypeStruct(panel_one.shape, BF16),
                jax.ShapeDtypeStruct(square, BF16),
                jax.ShapeDtypeStruct(panel_two.shape, BF16),
                jax.ShapeDtypeStruct(square, BF16),
                jax.ShapeDtypeStruct(square, BF16),
            ),
            in_specs=[hbm] * 9,
            out_specs=[vmem] * 5,
            scratch_shapes=[
                pltpu.VMEM(panel_one.shape, BF16),
                pltpu.VMEM(panel_two.shape, BF16),
                pltpu.SMEM(anc_one.shape, jnp.int32),
                pltpu.SMEM(anc_two.shape, jnp.int32),
                pltpu.SMEM(widths.shape, jnp.int32),
                pltpu.VMEM(inverse.shape, BF16),
                pltpu.VMEM(square, BF16),
                pltpu.VMEM(square, BF16),
                pltpu.VMEM(square, BF16),
                pltpu.VMEM((depth, PIECES, share, width), BF16),
                pltpu.VMEM((PIECES, share, width), BF16),
                pltpu.VMEM((PIECES, 2, depth, share, width), BF16),
                pltpu.VMEM((PIECES, width, width), F32),
                pltpu.VMEM((depth, PIECES, share, width), BF16),
                pltpu.VMEM((depth, PIECES, share, width), BF16),
                pltpu.VMEM((3, width, width), BF16),
                pltpu.VMEM((3, width, width), BF16),
                pltpu.VMEM((3, width, width), F32),
                pltpu.VMEM((3, n, rows, width), BF16),
                pltpu.VMEM((3, n, rows, width), BF16),
                pltpu.VMEM((3, rows, width), F32),
                pltpu.VMEM((3, owners, rows // owners, width), BF16),
                pltpu.VMEM((3, depth, rows // owners, width), BF16),
                pltpu.VMEM((2, 3, width, width), BF16),
                dma((9,)),
                dma((2, PIECES)),
                dma((2, max(depth, PIECES))),
                dma((chunks, n)),
                dma((PIECES, chunks)),
                dma((PIECES, chunks)),
                dma((PIECES, chunks)),
                dma((2, depth)),
                dma((2, 2, depth)),
                dma((2, 3)),
                dma((2, 3, n)),
                dma((2, 3, depth)),
                dma((2, 3, depth)),
                dma((2, 3, n)),
                dma((2, 3, n)),
            ],
            compiler_params=pltpu.CompilerParams(
                collective_id=0, has_side_effects=True, vmem_limit_bytes=60 * 1024 * 1024
            ),
            cost_estimate=pl.CostEstimate(flops=10**9, bytes_accessed=3 * 10**6, transcendentals=0),
        )(panel_one, panel_two, anc_one, anc_two, widths, inverse, diag_one, diag_two, link_two)
        return pl.pallas_call(
            hand_over,
            out_shape=tuple(jax.ShapeDtypeStruct(r.shape, r.dtype) for r in results),
            in_specs=[hbm] * 5,
            out_specs=[hbm] * 5,
            scratch_shapes=[pltpu.VMEM(r.shape, r.dtype) for r in results] + [dma((2, 5))],
            compiler_params=pltpu.CompilerParams(vmem_limit_bytes=60 * 1024 * 1024),
        )(*results)

    in_specs = (
        P("row", "col"),
        P(("row", "col"), None),
        P(),
        P(),
        P(("row", "col"), None),
        P(),
        P(),
        P(),
        P(),
    )
    out_specs = (P(("row", "col"), None), P(), P(("row", "col"), None), P(), P())
    return jax.shard_map(local, mesh=mesh, in_specs=in_specs, out_specs=out_specs, check_vma=False)
```

```python
import functools

import jax
import jax.numpy as jnp
from jax import lax
from jax.experimental import pallas as pl
from jax.experimental.pallas import tpu as pltpu
from jax.sharding import PartitionSpec as P

MESH = pl.DeviceIdType.MESH
PIECES = 4
F32 = jnp.float32
BF16 = jnp.bfloat16


def left_t(a, b):
    return lax.dot_general(a, b, (((0,), (0,)), ((), ())), preferred_element_type=F32)


def hand_over(*refs):
    sources, targets, held, sem = refs[:5], refs[5:10], refs[10:15], refs[15]
    loads = [pltpu.make_async_copy(sources[i], held[i], sem.at[0, i]) for i in range(5)]
    stores = [pltpu.make_async_copy(held[i], targets[i], sem.at[1, i]) for i in range(5)]
    for copy in loads:
        copy.start()
    for load, store in zip(loads, stores):
        load.wait()
        store.start()
    for copy in stores:
        copy.wait()


def kernel(
    n,
    depth,
    panel_one_hbm,
    panel_two_hbm,
    anc_one_hbm,
    anc_two_hbm,
    widths_hbm,
    inv_hbm,
    diag_one_hbm,
    diag_two_hbm,
    link_hbm,
    col_one_out,
    block_one_out,
    col_two_out,
    parent_out,
    block_two_out,
    panel_one,
    panel_two,
    anc_one,
    anc_two,
    widths,
    inv,
    diag_one,
    diag_two,
    link,
    lines,
    relay,
    panels,
    prod,
    prod_send,
    prod_recv,
    pair_send,
    pair_recv,
    sums,
    plane_send,
    plane_recv,
    part,
    line_send,
    line_recv,
    whole,
    fresh,
    load_sem,
    a_sem,
    b_sem,
    c_send,
    c_recv,
    f_send,
    f_recv,
    l_sem,
    p_sem,
    pair_sem,
    ps_sem,
    ls_sem,
    lg_sem,
    pg_sem,
    fg_sem,
):
    width = diag_one.shape[-1]
    share = panel_one.shape[0]
    small = n == PIECES
    row = lax.axis_index("row")
    z = lax.axis_index("col")
    chip = row // 2
    core = row % 2
    mine = chip % PIECES
    group = chip - mine
    z_group = z - z % PIECES
    sibling = (2 * chip + (1 - core), z)

    def on_chip(c):
        return (2 * c + core, z)

    def on_line(level):
        return (row, level)

    def send(src, dst, ssem, rsem, target):
        copy = pltpu.make_async_remote_copy(
            src_ref=src, dst_ref=dst, send_sem=ssem, recv_sem=rsem, device_id=target, device_id_type=MESH
        )
        copy.start()
        return copy

    def arrived(dst, rsem):
        pltpu.make_async_copy(dst, dst, rsem).wait()

    loads = []
    pairs = (
        (anc_one_hbm, anc_one),
        (anc_two_hbm, anc_two),
        (widths_hbm, widths),
        (panel_one_hbm, panel_one),
        (panel_two_hbm, panel_two),
        (inv_hbm, inv),
        (link_hbm, link),
        (diag_one_hbm, diag_one),
        (diag_two_hbm, diag_two),
    )
    for i, (src, dst) in enumerate(pairs):
        loads.append(pltpu.make_async_copy(src, dst, load_sem.at[i]))
        loads[-1].start()

    barrier = pltpu.get_barrier_semaphore()
    pl.semaphore_signal(barrier, inc=1, device_id=sibling, device_id_type=MESH)
    for i in range(1, n):
        pl.semaphore_signal(barrier, inc=1, device_id=on_chip((chip + i) % n), device_id_type=MESH)
    for i in range(1, depth):
        pl.semaphore_signal(barrier, inc=1, device_id=on_line((z + i) % depth), device_id_type=MESH)

    for copy in loads[:5]:
        copy.wait()
    columns = lax.broadcasted_iota(jnp.int32, (share, width), 1)
    member = []
    for p in range(PIECES):
        ancestors, s = (anc_one, p) if p < 2 else (anc_two, p - 2)
        found = jnp.int32(0)
        for t in range(ancestors.shape[1]):
            found += jnp.where(ancestors[s, t] == row, 1, 0).astype(jnp.int32)
        member.append(found.astype(F32))
        source = panel_one if p < 2 else panel_two
        values = source[:, s * width : (s + 1) * width]
        kept = jnp.where(columns < widths[p] * found, values.astype(F32), 0.0).astype(BF16)
        lines[z, p] = kept
    relay[mine] = lines[z, mine]

    pl.semaphore_wait(barrier, 1 + (n - 1) + (depth - 1))

    sent = []
    copies = []
    for i in range(1, PIECES):
        p = (mine + i) % PIECES
        copies.append(
            send(lines.at[z, p], relay.at[mine], a_sem.at[0, i], a_sem.at[1, i], on_chip(group + p))
        )
    for copy in copies:
        copy.wait_recv()
    sent += copies
    is_relay = group == z_group

    def local_piece():
        panels[mine, core, z] = relay[z % PIECES]

    if small:
        local_piece()
        first = None
    else:
        first = pltpu.make_async_remote_copy(
            src_ref=relay.at[z % PIECES],
            dst_ref=panels.at[mine, core, z],
            send_sem=b_sem.at[0, 0],
            recv_sem=b_sem.at[1, z],
            device_id=on_line(group + z % PIECES),
            device_id_type=MESH,
        )
        pl.when(is_relay)(local_piece)
        pl.when(jnp.logical_not(is_relay))(first.start)
    for i in range(1, PIECES):
        j = (z + i) % PIECES
        sent.append(
            send(relay.at[j], panels.at[mine, core, z], b_sem.at[0, i], b_sem.at[1, z], on_line(group + j))
        )
    line_copies = []

    def share_line():
        for i in range(1, depth):
            line_copies.append(
                send(
                    lines.at[z, 2:4], lines.at[z, 2:4], l_sem.at[0, i], l_sem.at[1, z], on_line((z + i) % depth)
                )
            )

    chunks = [(z + i) % depth for i in range(depth)] if small else [None]

    def chunk(p, c, level):
        return panels.at[p, c] if level is None else panels.at[p, c, level]

    def slot(level):
        return 0 if level is None else level

    def spread(start):
        for t, level in enumerate(chunks):
            if start:
                if level is None:
                    for i in range(1, depth):
                        other = (z + i) % depth
                        arrived(panels.at[mine, core, other], b_sem.at[1, other])
                elif t > 0:
                    arrived(panels.at[mine, core, level], b_sem.at[1, level])
            here = chunk(mine, core, level)
            targets = [(on_chip((chip + i) % n), c_recv) for i in range(1, n)] + [(sibling, f_recv)]
            for i, (target, rsem) in enumerate(targets):
                copy = pltpu.make_async_remote_copy(
                    src_ref=here,
                    dst_ref=here,
                    send_sem=c_send.at[t, i],
                    recv_sem=rsem.at[mine, slot(level)],
                    device_id=target,
                    device_id_type=MESH,
                )
                if start:
                    copy.start()
                else:
                    copy.wait_send()

    if small:
        spread(True)
    else:
        pl.when(is_relay)(functools.partial(spread, True))
    share_line()

    def forward(p, start):
        for t, level in enumerate(chunks):
            here = chunk(p, core, level)
            if start:
                arrived(here, c_recv.at[p, slot(level)])
            copy = pltpu.make_async_remote_copy(
                src_ref=here,
                dst_ref=here,
                send_sem=f_send.at[p, t],
                recv_sem=f_recv.at[p, slot(level)],
                device_id=sibling,
                device_id_type=MESH,
            )
            if start:
                copy.start()
            else:
                copy.wait_send()

    if not small:
        pl.when(jnp.logical_not(is_relay))(functools.partial(forward, mine, True))
    if small:
        for t, level in enumerate(chunks):
            for i in range(1, PIECES):
                p = (mine + i) % PIECES
                here = chunk(p, core, level)
                arrived(here, c_recv.at[p, level])
                sent.append(send(here, here, f_send.at[p, t], f_recv.at[p, level], sibling))
    else:
        for i in range(1, PIECES):
            forward((mine + i) % PIECES, True)
    for copy in loads[5:]:
        copy.wait()
    for p in range(PIECES):
        for level in range(depth if small else 1):
            arrived(chunk(p, 1 - core, level if small else None), f_recv.at[p, level])

    def send_products(half):
        for i in range(1, depth):
            other = (z + i) % depth
            sent.append(
                send(
                    prod_send.at[other, 2 * half : 2 * half + 2],
                    prod_recv.at[z, 2 * half : 2 * half + 2],
                    p_sem.at[0, half, i],
                    p_sem.at[1, half, z],
                    on_line(other),
                )
            )

    for p in range(PIECES):
        stacked = panels[p].reshape(2 * depth * share, width)
        product = jnp.dot(inv[...], stacked, preferred_element_type=F32) * member[p]
        prod[p] = product
        prod_send[:, p] = product.astype(BF16).reshape(depth, share, width)
        if p % 2 == 1:
            send_products(p // 2)
    for i in range(1, depth):
        other = (z + i) % depth
        arrived(lines.at[other, 2:4], l_sem.at[1, other])

    def inner(s, m):
        if m == 2:
            lower = lines[:, 2 + s].reshape(depth * share, width)
            return left_t(lower, prod_send[:, 2 + s].reshape(depth * share, width))
        return left_t(lines[z, 2 * m + s], fresh[s])

    rows = width // n
    owners = line_send.shape[1]
    owned = rows // owners
    every = owners == depth
    first_row = pl.multiple_of(chip * rows, rows)

    def pair_start(m):
        pair_send[m] = inner(1 - core, m).astype(BF16)
        sent.append(send(pair_send.at[m], pair_recv.at[m], pair_sem.at[0, m], pair_sem.at[1, m], sibling))

    def plane_start(m):
        value = inner(core, m)
        arrived(pair_recv.at[m], pair_sem.at[1, m])
        value += pair_recv[m].astype(F32)
        sums[m] = value
        plane_send[m] = value.astype(BF16).reshape(n, rows, width)
        for i in range(1, n):
            other = (chip + i) % n
            sent.append(
                send(
                    plane_send.at[m, other],
                    plane_recv.at[m, chip],
                    ps_sem.at[0, m, i],
                    ps_sem.at[1, m, chip],
                    on_chip(other),
                )
            )

    def reduce_copy(m, t, i):
        return pltpu.make_async_remote_copy(
            src_ref=line_send.at[m, t],
            dst_ref=line_recv.at[m, z],
            send_sem=ls_sem.at[0, m, i],
            recv_sem=ls_sem.at[1, m, z],
            device_id=on_line(t),
            device_id_type=MESH,
        )

    def to_owners(m, start):
        for t in range(owners):
            copy = reduce_copy(m, t, t)
            pl.when(z != t)(copy.start if start else copy.wait_send)

    def line_start(m):
        value = sums[m, pl.ds(first_row, rows)]
        for i in range(1, n):
            other = (chip + i) % n
            arrived(plane_recv.at[m, other], ps_sem.at[1, m, other])
            value += plane_recv[m, other].astype(F32)
        part[m] = value
        line_send[m] = value.astype(BF16).reshape(owners, owned, width)
        if every:
            for i in range(1, depth):
                copy = reduce_copy(m, (z + i) % depth, i)
                copy.start()
                sent.append(copy)
        else:
            to_owners(m, True)

    def owned_rows(level):
        return pl.ds(pl.multiple_of(chip * rows + level * owned, owned), owned)

    def gather_copy(m, i):
        here = whole.at[core, m, owned_rows(z), :]
        return pltpu.make_async_remote_copy(
            src_ref=here,
            dst_ref=here,
            send_sem=lg_sem.at[0, m, i],
            recv_sem=lg_sem.at[1, m, z],
            device_id=on_line((z + i) % depth),
            device_id_type=MESH,
        )

    def own(m):
        value = part[m, pl.ds(pl.multiple_of(z * owned, owned), owned)]
        for i in range(1, depth):
            other = (z + i) % depth
            arrived(line_recv.at[m, other], ls_sem.at[1, m, other])
            value += line_recv[m, other].astype(F32)
        if m == 0:
            limit = widths[core]
            at = chip * rows + z * owned + lax.broadcasted_iota(jnp.int32, (owned, width), 0)
            across = lax.broadcasted_iota(jnp.int32, (owned, width), 1)
            pivot = diag_one[core, owned_rows(z)].astype(F32)
            value = jnp.where((at < limit) & (across < limit), pivot, 0.0) - value
        whole[core, m, owned_rows(z)] = value.astype(BF16)
        for i in range(1, depth):
            gather_copy(m, i).start()

    def own_end(m):
        for i in range(1, depth):
            gather_copy(m, i).wait_send()

    def owners_only(f, m):
        if every:
            f(m)
        else:
            pl.when(z < owners)(functools.partial(f, m))

    def chip_rows(c, s, m):
        return whole.at[s, m, pl.ds(pl.multiple_of(c * rows, rows), rows), :]

    def back_start(m):
        if every:
            for i in range(1, depth):
                level = (z + i) % depth
                arrived(whole.at[core, m, owned_rows(level), :], lg_sem.at[1, m, level])
        else:
            for t in range(owners):
                there = whole.at[core, m, owned_rows(t), :]
                pl.when(z != t)(functools.partial(arrived, there, lg_sem.at[1, m, t]))
        here = chip_rows(chip, core, m)
        for i in range(1, n):
            sent.append(send(here, here, pg_sem.at[0, m, i], pg_sem.at[1, m, chip], on_chip((chip + i) % n)))
        sent.append(send(here, here, fg_sem.at[0, m, chip], fg_sem.at[1, m, chip], sibling))

    def back_forward(m):
        for i in range(1, n):
            other = (chip + i) % n
            there = chip_rows(other, core, m)
            arrived(there, pg_sem.at[1, m, other])
            sent.append(send(there, there, fg_sem.at[0, m, other], fg_sem.at[1, m, other], sibling))

    def masked_link(s):
        at = lax.broadcasted_iota(jnp.int32, (width, width), 0)
        across = lax.broadcasted_iota(jnp.int32, (width, width), 1)
        kept = (at < widths[s]) & (across < widths[2 + s])
        return jnp.where(kept, link[s].astype(F32), 0.0).astype(BF16)

    def total(p):
        value = prod[p, pl.ds(pl.multiple_of(z * share, share), share)]
        for i in range(1, depth):
            value += prod_recv[(z + i) % depth, p].astype(F32)
        return value

    def products_arrived(half):
        for i in range(1, depth):
            other = (z + i) % depth
            arrived(prod_recv.at[other, 2 * half : 2 * half + 2], p_sem.at[1, half, other])

    pair_start(2)
    plane_start(2)
    links = [masked_link(s) for s in range(2)]
    products_arrived(0)
    for s in range(2):
        new = (-total(s)).astype(BF16)
        fresh[s] = new
        col_one_out[:, s * width : (s + 1) * width] = new
    pair_start(0)
    pair_start(1)
    line_start(2)
    plane_start(0)
    plane_start(1)
    owners_only(own, 2)
    line_start(0)
    line_start(1)
    back_start(2)
    owners_only(own, 0)
    owners_only(own, 1)
    back_forward(2)
    back_start(0)
    back_start(1)
    products_arrived(1)
    for s in range(2):
        second = total(2 + s) + jnp.dot(fresh[s], links[s], preferred_element_type=F32)
        col_two_out[:, s * width : (s + 1) * width] = (-(second * member[2 + s])).astype(BF16)
    back_forward(0)
    back_forward(1)
    for m in range(3):
        for c in range(n):
            arrived(chip_rows(c, 1 - core, m), fg_sem.at[1, m, c])

    for s in range(2):
        block = whole[s, 0]
        cross = whole[s, 1]
        block_one_out[s] = block
        parent = -cross.astype(F32).T - jnp.dot(block, links[s], preferred_element_type=F32)
        parent = parent.astype(BF16)
        parent_out[s] = parent
        at = lax.broadcasted_iota(jnp.int32, (width, width), 0)
        across = lax.broadcasted_iota(jnp.int32, (width, width), 1)
        limit = widths[2 + s]
        value = jnp.where((at < limit) & (across < limit), diag_two[s].astype(F32), 0.0)
        value += whole[s, 2].astype(F32)
        value += jnp.dot(cross, links[s], preferred_element_type=F32)
        value -= left_t(links[s], parent)
        block_two_out[s] = value.astype(BF16)

    for copy in sent + line_copies:
        copy.wait_send()
    if small:
        spread(False)
    else:
        pl.when(jnp.logical_not(is_relay))(first.wait_send)
        pl.when(is_relay)(functools.partial(spread, False))
        pl.when(jnp.logical_not(is_relay))(functools.partial(forward, mine, False))
        for i in range(1, PIECES):
            forward((mine + i) % PIECES, False)
    for m in range(3):
        if not every:
            to_owners(m, False)
        owners_only(own_end, m)


def solution(mesh):
    n = mesh.shape["row"] // 2
    depth = mesh.shape["col"]

    def local(inverse, panel_one, anc_one, diag_one, panel_two, link_two, anc_two, diag_two, widths):
        width = diag_one.shape[-1]
        share = panel_one.shape[0]
        rows = width // n
        owners = max(1, min(depth, rows // 16))
        assert inverse.shape == (width, 2 * width) and n == depth and n % PIECES == 0
        assert share * depth == width and panel_one.shape[1] == 2 * width
        chunks = depth if n == PIECES else 1
        vmem = pl.BlockSpec(memory_space=pltpu.VMEM)
        hbm = pl.BlockSpec(memory_space=pl.ANY)
        dma = pltpu.SemaphoreType.DMA
        square = (2, width, width)
        results = pl.pallas_call(
            functools.partial(kernel, n, depth),
            out_shape=(
                jax.ShapeDtypeStruct(panel_one.shape, BF16),
                jax.ShapeDtypeStruct(square, BF16),
                jax.ShapeDtypeStruct(panel_two.shape, BF16),
                jax.ShapeDtypeStruct(square, BF16),
                jax.ShapeDtypeStruct(square, BF16),
            ),
            in_specs=[hbm] * 9,
            out_specs=[vmem] * 5,
            scratch_shapes=[
                pltpu.VMEM(panel_one.shape, BF16),
                pltpu.VMEM(panel_two.shape, BF16),
                pltpu.SMEM(anc_one.shape, jnp.int32),
                pltpu.SMEM(anc_two.shape, jnp.int32),
                pltpu.SMEM(widths.shape, jnp.int32),
                pltpu.VMEM(inverse.shape, BF16),
                pltpu.VMEM(square, BF16),
                pltpu.VMEM(square, BF16),
                pltpu.VMEM(square, BF16),
                pltpu.VMEM((depth, PIECES, share, width), BF16),
                pltpu.VMEM((PIECES, share, width), BF16),
                pltpu.VMEM((PIECES, 2, depth, share, width), BF16),
                pltpu.VMEM((PIECES, width, width), F32),
                pltpu.VMEM((depth, PIECES, share, width), BF16),
                pltpu.VMEM((depth, PIECES, share, width), BF16),
                pltpu.VMEM((3, width, width), BF16),
                pltpu.VMEM((3, width, width), BF16),
                pltpu.VMEM((3, width, width), F32),
                pltpu.VMEM((3, n, rows, width), BF16),
                pltpu.VMEM((3, n, rows, width), BF16),
                pltpu.VMEM((3, rows, width), F32),
                pltpu.VMEM((3, owners, rows // owners, width), BF16),
                pltpu.VMEM((3, depth, rows // owners, width), BF16),
                pltpu.VMEM((2, 3, width, width), BF16),
                pltpu.VMEM((2, share, width), BF16),
                dma((9,)),
                dma((2, PIECES)),
                dma((2, max(depth, PIECES))),
                dma((chunks, n)),
                dma((PIECES, chunks)),
                dma((PIECES, chunks)),
                dma((PIECES, chunks)),
                dma((2, depth)),
                dma((2, 2, depth)),
                dma((2, 3)),
                dma((2, 3, n)),
                dma((2, 3, depth)),
                dma((2, 3, depth)),
                dma((2, 3, n)),
                dma((2, 3, n)),
            ],
            compiler_params=pltpu.CompilerParams(
                collective_id=0, has_side_effects=True, vmem_limit_bytes=60 * 1024 * 1024
            ),
            cost_estimate=pl.CostEstimate(flops=10**9, bytes_accessed=3 * 10**6, transcendentals=0),
        )(panel_one, panel_two, anc_one, anc_two, widths, inverse, diag_one, diag_two, link_two)
        return pl.pallas_call(
            hand_over,
            out_shape=tuple(jax.ShapeDtypeStruct(r.shape, r.dtype) for r in results),
            in_specs=[hbm] * 5,
            out_specs=[hbm] * 5,
            scratch_shapes=[pltpu.VMEM(r.shape, r.dtype) for r in results] + [dma((2, 5))],
            compiler_params=pltpu.CompilerParams(vmem_limit_bytes=60 * 1024 * 1024),
        )(*results)

    in_specs = (
        P("row", "col"),
        P(("row", "col"), None),
        P(),
        P(),
        P(("row", "col"), None),
        P(),
        P(),
        P(),
        P(),
    )
    out_specs = (P(("row", "col"), None), P(), P(("row", "col"), None), P(), P())
    return jax.shard_map(local, mesh=mesh, in_specs=in_specs, out_specs=out_specs, check_vma=False)
```

```python
import functools

import jax
import jax.numpy as jnp
from jax import lax
from jax.experimental import pallas as pl
from jax.experimental.pallas import tpu as pltpu
from jax.sharding import PartitionSpec as P

MESH = pl.DeviceIdType.MESH
PIECES = 4
F32 = jnp.float32
BF16 = jnp.bfloat16


def left_t(a, b):
    return lax.dot_general(a, b, (((0,), (0,)), ((), ())), preferred_element_type=F32)


def hand_over(*refs):
    sources, targets, held, sem = refs[:5], refs[5:10], refs[10:15], refs[15]
    loads = [pltpu.make_async_copy(sources[i], held[i], sem.at[0, i]) for i in range(5)]
    stores = [pltpu.make_async_copy(held[i], targets[i], sem.at[1, i]) for i in range(5)]
    for copy in loads:
        copy.start()
    for load, store in zip(loads, stores):
        load.wait()
        store.start()
    for copy in stores:
        copy.wait()


def kernel(
    n,
    depth,
    panel_one_hbm,
    panel_two_hbm,
    anc_one_hbm,
    anc_two_hbm,
    widths_hbm,
    inv_hbm,
    diag_one_hbm,
    diag_two_hbm,
    link_hbm,
    col_one_out,
    block_one_out,
    col_two_out,
    parent_out,
    block_two_out,
    panel_one,
    panel_two,
    anc_one,
    anc_two,
    widths,
    inv,
    diag_one,
    diag_two,
    link,
    lines,
    relay,
    panels,
    prod,
    prod_send,
    prod_recv,
    pair_send,
    pair_recv,
    sums,
    plane_send,
    plane_recv,
    part,
    line_send,
    line_recv,
    whole,
    fresh,
    load_sem,
    a_sem,
    b_sem,
    c_send,
    c_recv,
    f_send,
    f_recv,
    l_sem,
    p_sem,
    pair_sem,
    ps_sem,
    ls_sem,
    lg_sem,
    pg_sem,
    fg_sem,
):
    width = diag_one.shape[-1]
    share = panel_one.shape[0]
    small = n == PIECES
    row = lax.axis_index("row")
    z = lax.axis_index("col")
    chip = row // 2
    core = row % 2
    mine = chip % PIECES
    group = chip - mine
    z_group = z - z % PIECES
    sibling = (2 * chip + (1 - core), z)

    def on_chip(c):
        return (2 * c + core, z)

    def on_line(level):
        return (row, level)

    def send(src, dst, ssem, rsem, target):
        copy = pltpu.make_async_remote_copy(
            src_ref=src, dst_ref=dst, send_sem=ssem, recv_sem=rsem, device_id=target, device_id_type=MESH
        )
        copy.start()
        return copy

    def arrived(dst, rsem):
        pltpu.make_async_copy(dst, dst, rsem).wait()

    loads = []
    pairs = (
        (anc_one_hbm, anc_one),
        (anc_two_hbm, anc_two),
        (widths_hbm, widths),
        (panel_one_hbm, panel_one),
        (panel_two_hbm, panel_two),
        (inv_hbm, inv),
        (link_hbm, link),
        (diag_one_hbm, diag_one),
        (diag_two_hbm, diag_two),
    )
    for i, (src, dst) in enumerate(pairs):
        loads.append(pltpu.make_async_copy(src, dst, load_sem.at[i]))
        loads[-1].start()

    barrier = pltpu.get_barrier_semaphore()
    pl.semaphore_signal(barrier, inc=1, device_id=sibling, device_id_type=MESH)
    for i in range(1, n):
        pl.semaphore_signal(barrier, inc=1, device_id=on_chip((chip + i) % n), device_id_type=MESH)
    for i in range(1, depth):
        pl.semaphore_signal(barrier, inc=1, device_id=on_line((z + i) % depth), device_id_type=MESH)

    for copy in loads[:5]:
        copy.wait()
    columns = lax.broadcasted_iota(jnp.int32, (share, width), 1)
    member = []
    for p in range(PIECES):
        ancestors, s = (anc_one, p) if p < 2 else (anc_two, p - 2)
        found = jnp.int32(0)
        for t in range(ancestors.shape[1]):
            found += jnp.where(ancestors[s, t] == row, 1, 0).astype(jnp.int32)
        member.append(found.astype(F32))
        source = panel_one if p < 2 else panel_two
        values = source[:, s * width : (s + 1) * width]
        kept = jnp.where(columns < widths[p] * found, values.astype(F32), 0.0).astype(BF16)
        lines[z, p] = kept
    relay[mine] = lines[z, mine]

    pl.semaphore_wait(barrier, 1 + (n - 1) + (depth - 1))

    sent = []
    copies = []
    for i in range(1, PIECES):
        p = (mine + i) % PIECES
        copies.append(
            send(lines.at[z, p], relay.at[mine], a_sem.at[0, i], a_sem.at[1, i], on_chip(group + p))
        )
    for copy in copies:
        copy.wait_recv()
    sent += copies
    is_relay = group == z_group

    def local_piece():
        panels[mine, core, z] = relay[z % PIECES]

    if small:
        local_piece()
        first = None
    else:
        first = pltpu.make_async_remote_copy(
            src_ref=relay.at[z % PIECES],
            dst_ref=panels.at[mine, core, z],
            send_sem=b_sem.at[0, 0],
            recv_sem=b_sem.at[1, z],
            device_id=on_line(group + z % PIECES),
            device_id_type=MESH,
        )
        pl.when(is_relay)(local_piece)
        pl.when(jnp.logical_not(is_relay))(first.start)
    for i in range(1, PIECES):
        j = (z + i) % PIECES
        sent.append(
            send(relay.at[j], panels.at[mine, core, z], b_sem.at[0, i], b_sem.at[1, z], on_line(group + j))
        )
    line_copies = []

    def share_line():
        for i in range(1, depth):
            line_copies.append(
                send(
                    lines.at[z, 2:4], lines.at[z, 2:4], l_sem.at[0, i], l_sem.at[1, z], on_line((z + i) % depth)
                )
            )

    chunks = [(z + i) % depth for i in range(depth)] if small else [None]

    def chunk(p, c, level):
        return panels.at[p, c] if level is None else panels.at[p, c, level]

    def slot(level):
        return 0 if level is None else level

    def spread(start):
        for t, level in enumerate(chunks):
            if start:
                if level is None:
                    for i in range(1, depth):
                        other = (z + i) % depth
                        arrived(panels.at[mine, core, other], b_sem.at[1, other])
                elif t > 0:
                    arrived(panels.at[mine, core, level], b_sem.at[1, level])
            here = chunk(mine, core, level)
            targets = [(on_chip((chip + i) % n), c_recv) for i in range(1, n)] + [(sibling, f_recv)]
            for i, (target, rsem) in enumerate(targets):
                copy = pltpu.make_async_remote_copy(
                    src_ref=here,
                    dst_ref=here,
                    send_sem=c_send.at[t, i],
                    recv_sem=rsem.at[mine, slot(level)],
                    device_id=target,
                    device_id_type=MESH,
                )
                if start:
                    copy.start()
                else:
                    copy.wait_send()

    if small:
        spread(True)
    else:
        pl.when(is_relay)(functools.partial(spread, True))
    share_line()

    def forward(p, start):
        for t, level in enumerate(chunks):
            here = chunk(p, core, level)
            if start:
                arrived(here, c_recv.at[p, slot(level)])
            copy = pltpu.make_async_remote_copy(
                src_ref=here,
                dst_ref=here,
                send_sem=f_send.at[p, t],
                recv_sem=f_recv.at[p, slot(level)],
                device_id=sibling,
                device_id_type=MESH,
            )
            if start:
                copy.start()
            else:
                copy.wait_send()

    if not small:
        pl.when(jnp.logical_not(is_relay))(functools.partial(forward, mine, True))
    if small:
        for t, level in enumerate(chunks):
            for i in range(1, PIECES):
                p = (mine + i) % PIECES
                here = chunk(p, core, level)
                arrived(here, c_recv.at[p, level])
                sent.append(send(here, here, f_send.at[p, t], f_recv.at[p, level], sibling))
    else:
        for i in range(1, PIECES):
            forward((mine + i) % PIECES, True)
    for copy in loads[5:]:
        copy.wait()
    for p in range(PIECES):
        for level in range(depth if small else 1):
            arrived(chunk(p, 1 - core, level if small else None), f_recv.at[p, level])

    def send_products(half):
        for i in range(1, depth):
            other = (z + i) % depth
            sent.append(
                send(
                    prod_send.at[other, 2 * half : 2 * half + 2],
                    prod_recv.at[z, 2 * half : 2 * half + 2],
                    p_sem.at[0, half, i],
                    p_sem.at[1, half, z],
                    on_line(other),
                )
            )

    for p in range(PIECES):
        stacked = panels[p].reshape(2 * depth * share, width)
        product = jnp.dot(inv[...], stacked, preferred_element_type=F32) * member[p]
        prod[p] = product
        prod_send[:, p] = product.astype(BF16).reshape(depth, share, width)
        if p == 1:
            send_products(0)
    for i in range(1, depth):
        other = (z + i) % depth
        arrived(lines.at[other, 2:4], l_sem.at[1, other])

    def inner(s, m):
        if m == 2:
            lower = lines[:, 2 + s].reshape(depth * share, width)
            return left_t(lower, prod_send[:, 2 + s].reshape(depth * share, width))
        return left_t(lines[z, 2 * m + s], fresh[s])

    rows = width // n
    owners = line_send.shape[1]
    owned = rows // owners
    every = owners == depth
    first_row = pl.multiple_of(chip * rows, rows)

    def pair_start(m):
        pair_send[m] = inner(1 - core, m).astype(BF16)
        sent.append(send(pair_send.at[m], pair_recv.at[m], pair_sem.at[0, m], pair_sem.at[1, m], sibling))

    def plane_start(m):
        value = inner(core, m)
        arrived(pair_recv.at[m], pair_sem.at[1, m])
        value += pair_recv[m].astype(F32)
        sums[m] = value
        plane_send[m] = value.astype(BF16).reshape(n, rows, width)
        for i in range(1, n):
            other = (chip + i) % n
            sent.append(
                send(
                    plane_send.at[m, other],
                    plane_recv.at[m, chip],
                    ps_sem.at[0, m, i],
                    ps_sem.at[1, m, chip],
                    on_chip(other),
                )
            )

    def reduce_copy(m, t, i):
        return pltpu.make_async_remote_copy(
            src_ref=line_send.at[m, t],
            dst_ref=line_recv.at[m, z],
            send_sem=ls_sem.at[0, m, i],
            recv_sem=ls_sem.at[1, m, z],
            device_id=on_line(t),
            device_id_type=MESH,
        )

    def to_owners(m, start):
        for t in range(owners):
            copy = reduce_copy(m, t, t)
            pl.when(z != t)(copy.start if start else copy.wait_send)

    def line_start(m):
        value = sums[m, pl.ds(first_row, rows)]
        for i in range(1, n):
            other = (chip + i) % n
            arrived(plane_recv.at[m, other], ps_sem.at[1, m, other])
            value += plane_recv[m, other].astype(F32)
        part[m] = value
        line_send[m] = value.astype(BF16).reshape(owners, owned, width)
        if every:
            for i in range(1, depth):
                copy = reduce_copy(m, (z + i) % depth, i)
                copy.start()
                sent.append(copy)
        else:
            to_owners(m, True)

    def owned_rows(level):
        return pl.ds(pl.multiple_of(chip * rows + level * owned, owned), owned)

    def gather_copy(m, i):
        here = whole.at[core, m, owned_rows(z), :]
        return pltpu.make_async_remote_copy(
            src_ref=here,
            dst_ref=here,
            send_sem=lg_sem.at[0, m, i],
            recv_sem=lg_sem.at[1, m, z],
            device_id=on_line((z + i) % depth),
            device_id_type=MESH,
        )

    def own(m):
        value = part[m, pl.ds(pl.multiple_of(z * owned, owned), owned)]
        for i in range(1, depth):
            other = (z + i) % depth
            arrived(line_recv.at[m, other], ls_sem.at[1, m, other])
            value += line_recv[m, other].astype(F32)
        if m == 0:
            limit = widths[core]
            at = chip * rows + z * owned + lax.broadcasted_iota(jnp.int32, (owned, width), 0)
            across = lax.broadcasted_iota(jnp.int32, (owned, width), 1)
            pivot = diag_one[core, owned_rows(z)].astype(F32)
            value = jnp.where((at < limit) & (across < limit), pivot, 0.0) - value
        whole[core, m, owned_rows(z)] = value.astype(BF16)
        for i in range(1, depth):
            gather_copy(m, i).start()

    def own_end(m):
        for i in range(1, depth):
            gather_copy(m, i).wait_send()

    def owners_only(f, m):
        if every:
            f(m)
        else:
            pl.when(z < owners)(functools.partial(f, m))

    def chip_rows(c, s, m):
        return whole.at[s, m, pl.ds(pl.multiple_of(c * rows, rows), rows), :]

    def back_start(m):
        if every:
            for i in range(1, depth):
                level = (z + i) % depth
                arrived(whole.at[core, m, owned_rows(level), :], lg_sem.at[1, m, level])
        else:
            for t in range(owners):
                there = whole.at[core, m, owned_rows(t), :]
                pl.when(z != t)(functools.partial(arrived, there, lg_sem.at[1, m, t]))
        here = chip_rows(chip, core, m)
        for i in range(1, n):
            sent.append(send(here, here, pg_sem.at[0, m, i], pg_sem.at[1, m, chip], on_chip((chip + i) % n)))
        sent.append(send(here, here, fg_sem.at[0, m, chip], fg_sem.at[1, m, chip], sibling))

    def back_forward(m):
        for i in range(1, n):
            other = (chip + i) % n
            there = chip_rows(other, core, m)
            arrived(there, pg_sem.at[1, m, other])
            sent.append(send(there, there, fg_sem.at[0, m, other], fg_sem.at[1, m, other], sibling))

    def masked_link(s):
        at = lax.broadcasted_iota(jnp.int32, (width, width), 0)
        across = lax.broadcasted_iota(jnp.int32, (width, width), 1)
        kept = (at < widths[s]) & (across < widths[2 + s])
        return jnp.where(kept, link[s].astype(F32), 0.0).astype(BF16)

    def total(p):
        value = prod[p, pl.ds(pl.multiple_of(z * share, share), share)]
        for i in range(1, depth):
            value += prod_recv[(z + i) % depth, p].astype(F32)
        return value

    def products_arrived(half):
        for i in range(1, depth):
            other = (z + i) % depth
            arrived(prod_recv.at[other, 2 * half : 2 * half + 2], p_sem.at[1, half, other])

    pair_start(2)
    plane_start(2)
    links = [masked_link(s) for s in range(2)]
    products_arrived(0)
    send_products(1)
    for s in range(2):
        new = (-total(s)).astype(BF16)
        fresh[s] = new
        col_one_out[:, s * width : (s + 1) * width] = new
    pair_start(0)
    pair_start(1)
    line_start(2)
    plane_start(0)
    plane_start(1)
    owners_only(own, 2)
    line_start(0)
    line_start(1)
    back_start(2)
    owners_only(own, 0)
    owners_only(own, 1)
    back_forward(2)
    back_start(0)
    back_start(1)
    products_arrived(1)
    for s in range(2):
        second = total(2 + s) + jnp.dot(fresh[s], links[s], preferred_element_type=F32)
        col_two_out[:, s * width : (s + 1) * width] = (-(second * member[2 + s])).astype(BF16)
    back_forward(0)
    back_forward(1)
    for m in range(3):
        for c in range(n):
            arrived(chip_rows(c, 1 - core, m), fg_sem.at[1, m, c])

    for s in range(2):
        block = whole[s, 0]
        cross = whole[s, 1]
        block_one_out[s] = block
        parent = -cross.astype(F32).T - jnp.dot(block, links[s], preferred_element_type=F32)
        parent = parent.astype(BF16)
        parent_out[s] = parent
        at = lax.broadcasted_iota(jnp.int32, (width, width), 0)
        across = lax.broadcasted_iota(jnp.int32, (width, width), 1)
        limit = widths[2 + s]
        value = jnp.where((at < limit) & (across < limit), diag_two[s].astype(F32), 0.0)
        value += whole[s, 2].astype(F32)
        value += jnp.dot(cross, links[s], preferred_element_type=F32)
        value -= left_t(links[s], parent)
        block_two_out[s] = value.astype(BF16)

    for copy in sent + line_copies:
        copy.wait_send()
    if small:
        spread(False)
    else:
        pl.when(jnp.logical_not(is_relay))(first.wait_send)
        pl.when(is_relay)(functools.partial(spread, False))
        pl.when(jnp.logical_not(is_relay))(functools.partial(forward, mine, False))
        for i in range(1, PIECES):
            forward((mine + i) % PIECES, False)
    for m in range(3):
        if not every:
            to_owners(m, False)
        owners_only(own_end, m)


def solution(mesh):
    n = mesh.shape["row"] // 2
    depth = mesh.shape["col"]

    def local(inverse, panel_one, anc_one, diag_one, panel_two, link_two, anc_two, diag_two, widths):
        width = diag_one.shape[-1]
        share = panel_one.shape[0]
        rows = width // n
        owners = max(1, min(depth, rows // 16))
        assert inverse.shape == (width, 2 * width) and n == depth and n % PIECES == 0
        assert share * depth == width and panel_one.shape[1] == 2 * width
        chunks = depth if n == PIECES else 1
        vmem = pl.BlockSpec(memory_space=pltpu.VMEM)
        hbm = pl.BlockSpec(memory_space=pl.ANY)
        dma = pltpu.SemaphoreType.DMA
        square = (2, width, width)
        results = pl.pallas_call(
            functools.partial(kernel, n, depth),
            out_shape=(
                jax.ShapeDtypeStruct(panel_one.shape, BF16),
                jax.ShapeDtypeStruct(square, BF16),
                jax.ShapeDtypeStruct(panel_two.shape, BF16),
                jax.ShapeDtypeStruct(square, BF16),
                jax.ShapeDtypeStruct(square, BF16),
            ),
            in_specs=[hbm] * 9,
            out_specs=[vmem] * 5,
            scratch_shapes=[
                pltpu.VMEM(panel_one.shape, BF16),
                pltpu.VMEM(panel_two.shape, BF16),
                pltpu.SMEM(anc_one.shape, jnp.int32),
                pltpu.SMEM(anc_two.shape, jnp.int32),
                pltpu.SMEM(widths.shape, jnp.int32),
                pltpu.VMEM(inverse.shape, BF16),
                pltpu.VMEM(square, BF16),
                pltpu.VMEM(square, BF16),
                pltpu.VMEM(square, BF16),
                pltpu.VMEM((depth, PIECES, share, width), BF16),
                pltpu.VMEM((PIECES, share, width), BF16),
                pltpu.VMEM((PIECES, 2, depth, share, width), BF16),
                pltpu.VMEM((PIECES, width, width), F32),
                pltpu.VMEM((depth, PIECES, share, width), BF16),
                pltpu.VMEM((depth, PIECES, share, width), BF16),
                pltpu.VMEM((3, width, width), BF16),
                pltpu.VMEM((3, width, width), BF16),
                pltpu.VMEM((3, width, width), F32),
                pltpu.VMEM((3, n, rows, width), BF16),
                pltpu.VMEM((3, n, rows, width), BF16),
                pltpu.VMEM((3, rows, width), F32),
                pltpu.VMEM((3, owners, rows // owners, width), BF16),
                pltpu.VMEM((3, depth, rows // owners, width), BF16),
                pltpu.VMEM((2, 3, width, width), BF16),
                pltpu.VMEM((2, share, width), BF16),
                dma((9,)),
                dma((2, PIECES)),
                dma((2, max(depth, PIECES))),
                dma((chunks, n)),
                dma((PIECES, chunks)),
                dma((PIECES, chunks)),
                dma((PIECES, chunks)),
                dma((2, depth)),
                dma((2, 2, depth)),
                dma((2, 3)),
                dma((2, 3, n)),
                dma((2, 3, depth)),
                dma((2, 3, depth)),
                dma((2, 3, n)),
                dma((2, 3, n)),
            ],
            compiler_params=pltpu.CompilerParams(
                collective_id=0, has_side_effects=True, vmem_limit_bytes=60 * 1024 * 1024
            ),
            cost_estimate=pl.CostEstimate(flops=10**9, bytes_accessed=3 * 10**6, transcendentals=0),
        )(panel_one, panel_two, anc_one, anc_two, widths, inverse, diag_one, diag_two, link_two)
        return pl.pallas_call(
            hand_over,
            out_shape=tuple(jax.ShapeDtypeStruct(r.shape, r.dtype) for r in results),
            in_specs=[hbm] * 5,
            out_specs=[hbm] * 5,
            scratch_shapes=[pltpu.VMEM(r.shape, r.dtype) for r in results] + [dma((2, 5))],
            compiler_params=pltpu.CompilerParams(vmem_limit_bytes=60 * 1024 * 1024),
        )(*results)

    in_specs = (
        P("row", "col"),
        P(("row", "col"), None),
        P(),
        P(),
        P(("row", "col"), None),
        P(),
        P(),
        P(),
        P(),
    )
    out_specs = (P(("row", "col"), None), P(), P(("row", "col"), None), P(), P())
    return jax.shard_map(local, mesh=mesh, in_specs=in_specs, out_specs=out_specs, check_vma=False)
```
